256 devices in a mesh: section: 8 (over y, x_hi), rep: 32 (over z, x_lo, core).
Axes of the slice: x: 4 (x_hi: 2, x_lo: 2; x = x_hi * 2 + x_lo), y: 4, z: 8, core: 2. Of those that a mesh axis runs over, the one named last changes fastest.
Arguments:
- history: bfloat16 [8, 64, 64, 9216], P('section', 'rep'), may hold values from -6 to 6
- codes: int32 [8, 64, 64, 9216], P('section', 'rep'), may hold values from -128 to 127
- scales: float32 [8, 64, 64], P('section', 'rep'), may hold values from 0.003 to 0.03
- sample_ids: int32 [32, 2], P('rep'), may hold values from 0 to 1, each once within a row
- cotangent: bfloat16 [64, 64, 9216], P('rep'), may hold values from -6 to 6
- ln_gain: float32 [8, 9216], P('section'), may hold values from 0.5 to 1.5
- ln_bias: float32 [8, 9216], P('section'), may hold values from -3 to 3
- down_weight: bfloat16 [8, 9216, 256], P('section', 'rep'), may hold values from -0.1875 to 0.1875
- up_weight: bfloat16 [8, 9216, 256], P('section', 'rep'), may hold values from -0.0625 to 0.0625
Outputs:
- input_grads: bfloat16 [8, 64, 64, 9216], P('section', 'rep')
- adapter_grads: float32 [8, 9216, 512], P('section', 'rep')
The draws below stay inside these ranges and needn't reach their ends.
Inputs may be any that keep to these rules, and one draw needn't show every extreme that they name: `sample_ids`: each replica's row names every history entry of that replica once.
All inputs are finite; a program needn't handle non-finite values.
Results may differ from the reference program's by a relative error of at most 0.038.
Values may be sent and summed in bfloat16 or wider, within the bound.
A program may use at most 128 MiB of HBM per device.

```python
import math
import jax
import jax.numpy as jnp
from jax import lax

D = 9216
R = 256
MB = 2
TOK_MB = 64
N_SECTION = 8
N_REP = 32


def touch_ends(values, rng, smallest, high):
    index_at = [jax.random.randint(jax.random.fold_in(rng, axis), (), 0, length) for axis, length in enumerate(values.shape)]
    widest = values.shape.index(max(values.shape))
    neighbour = index_at[:widest] + [(index_at[widest] + 1) % values.shape[widest]] + index_at[widest + 1:]
    return values.at[tuple(index_at)].set(smallest).at[tuple(neighbour)].set(high)


def spiked(entries, stream_key, source, target, parts, factor):
    def block_of(position):
        return (jnp.arange(entries.shape[position]) // (entries.shape[position] // parts)).reshape((-1,) + (1,) * (entries.ndim - 1 - position))

    near = jax.random.permutation(stream_key, parts)[block_of(target)]
    second = (block_of(target) + parts // 2) % parts
    return jnp.where((block_of(source) == near) | (block_of(source) == second), factor * entries, entries)


def block_levels(stream_key, extent, shards, smallest, largest):
    gain, own = 1.0, jax.random.fold_in(stream_key, 6)
    for position, parts in shards:
        draws = jnp.exp(jax.random.uniform(jax.random.fold_in(own, position), (parts,), jnp.float32, smallest / len(shards), largest / len(shards)))
        gain = gain * jnp.repeat(draws, extent[position] // parts).reshape([-1 if axis == position else 1 for axis in range(len(extent))])
    return gain


def bell_draw(stream_key, extent, width, limit, split=(), kind=jnp.bfloat16):
    drawn = width * jax.random.normal(stream_key, extent, jnp.float32)
    if split:
        drawn = drawn * block_levels(stream_key, extent, split, -0.22, 0.18)
    return jnp.clip(drawn, -limit, limit).astype(kind)


def gaussian_with(own_key, shape, deviation, bound, shards, heavy, kind=jnp.bfloat16):
    array = deviation * jax.random.normal(own_key, shape, jnp.float32)
    if shards:
        array = array * block_levels(own_key, shape, shards, -0.22, 0.18)
    return jnp.clip(spiked(array, jax.random.fold_in(own_key, 3), *heavy), -bound, bound).astype(kind)


def setup_inputs(seed: int = 0) -> dict:
    streams_of = jax.random.split(jax.random.key(seed), 10)
    history = bell_draw(streams_of[0], (N_SECTION, N_REP * MB, TOK_MB, D), 1.0, 6.0, ((0, 8), (1, 32)))
    codes = touch_ends(jax.random.randint(streams_of[1], (N_SECTION, N_REP * MB, TOK_MB, D), -128, 128), jax.random.fold_in(streams_of[1], 1), -128, 127).astype(jnp.int32)
    scales = jnp.clip(jnp.exp(math.log(0.03) - 2.3025851 * jax.random.uniform(streams_of[2], (N_SECTION, N_REP * MB, TOK_MB), jnp.float32) ** block_levels(streams_of[2], (N_SECTION, N_REP * MB, TOK_MB), ((0, 8), (1, 32)), -0.2, 0.2)), 0.003, 0.03)
    sample_ids = jax.vmap(lambda own: jax.random.permutation(own, MB))(jax.random.split(streams_of[3], N_REP)).reshape((N_REP, MB)).astype(jnp.int32)
    cotangent = gaussian_with(streams_of[4], (N_REP * MB, TOK_MB, D), 1.0, 6.0, ((0, 32),), (0, 2, 32, 2.75))
    ln_gain = jnp.clip(1.0 + 0.1 * jax.random.normal(streams_of[5], (N_SECTION, D), jnp.float32), 0.5, 1.5)
    ln_bias = bell_draw(streams_of[6], (N_SECTION, D), 0.5, 3.0, ((0, 8),), jnp.float32)
    down_weight = bell_draw(streams_of[7], (N_SECTION, D, R), (D // 8) ** -0.5, 0.1875, ((0, 8), (1, 32)))
    up_weight = bell_draw(streams_of[8], (N_SECTION, D, R), D ** -0.5, 0.0625, ((0, 8), (1, 32)))
    return dict(history=history, codes=codes, scales=scales, sample_ids=sample_ids, cotangent=cotangent, ln_gain=ln_gain, ln_bias=ln_bias, down_weight=down_weight, up_weight=up_weight)


EPSILON = 1e-05
HALF_ROOT = 0.7071067811865476
DENSITY = 0.3989422804014327

def unpack_codes(levels):
    return levels.astype(jnp.float32)

def gelu_pair(preact):
    normal_cdf = 0.5 * (1.0 + lax.erf(preact * HALF_ROOT))
    bump = DENSITY * jnp.exp(-0.5 * preact * preact)
    return (preact * normal_cdf, normal_cdf + preact * bump)

def section_inputs(stored, packed, scaling, picks):
    chosen = jnp.take(stored, picks, axis=0).astype(jnp.float32)
    rebuilt = chosen + scaling[..., None] * unpack_codes(packed)
    return rebuilt.astype(jnp.bfloat16).reshape(-1, stored.shape[-1])

def normalize(inputs, gain_row, bias_row):
    values = inputs.astype(jnp.float32)
    centred = values - lax.optimization_barrier(jnp.mean(values, axis=-1, keepdims=True))
    inv_std = lax.rsqrt(lax.optimization_barrier(jnp.mean(centred * centred, axis=-1, keepdims=True)) + EPSILON)
    scaled = centred * inv_std
    normed = (scaled * gain_row + bias_row).astype(jnp.bfloat16)
    return (normed, scaled, inv_std)

def input_grad(out_grad, back, gain_row, scaled, inv_std):
    weighted = back * gain_row
    inner = weighted - lax.optimization_barrier(jnp.mean(weighted, axis=-1, keepdims=True)) - scaled * lax.optimization_barrier(jnp.mean(weighted * scaled, axis=-1, keepdims=True))
    return (out_grad.astype(jnp.float32) + inv_std * inner).astype(jnp.bfloat16)

def contract_rows(left, right):
    return lax.dot_general(left, right, (((0,), (0,)), ((), ())), preferred_element_type=jnp.float32)

def contract_cols(left, right):
    return lax.dot_general(left, right, (((1,), (1,)), ((), ())), preferred_element_type=jnp.float32)

def replica_backward(stored, packed, scaling, picks, out_grad, gain_row, bias_row, w_down, w_up):
    inputs = section_inputs(stored, packed, scaling, picks)
    normed, scaled, inv_std = normalize(inputs, gain_row, bias_row)
    activated, slopes = gelu_pair(jnp.dot(normed, w_down, preferred_element_type=jnp.float32))
    hidden = activated.astype(jnp.bfloat16)
    act_grad = (jnp.dot(out_grad, w_up, preferred_element_type=jnp.float32) * slopes).astype(jnp.bfloat16)
    back = contract_cols(act_grad, w_down)
    result = input_grad(out_grad, back, gain_row, scaled, inv_std)
    terms = jnp.concatenate([contract_rows(normed, act_grad), contract_rows(out_grad, hidden)], axis=1) / TOK_MB
    return (result, terms)

def reference(history, codes, scales, sample_ids, cotangent, ln_gain, ln_bias, down_weight, up_weight):
    stored = history.reshape(N_SECTION, N_REP, MB, TOK_MB, D)
    packed = codes.reshape(N_SECTION, N_REP, MB, TOK_MB, D)
    scaling = scales.reshape(N_SECTION, N_REP, MB, TOK_MB)
    start_grad = cotangent.reshape(N_REP, MB * TOK_MB, D)
    batched = jax.vmap(replica_backward, in_axes=(0, 0, 0, 0, 0, None, None, None, None))

    def per_section(out_grad, section_id):
        results, terms = batched(stored[section_id], packed[section_id], scaling[section_id], sample_ids, out_grad, ln_gain[section_id], ln_bias[section_id], down_weight[section_id], up_weight[section_id])
        rounded = lax.optimization_barrier(terms.astype(jnp.bfloat16))
        summed = lax.optimization_barrier(jnp.sum(rounded.astype(jnp.float32), axis=0))
        return (results, (results, summed))
    _, (grads_in, sums) = lax.scan(per_section, start_grad, jnp.arange(N_SECTION, dtype=jnp.int32), reverse=True)
    return (grads_in.reshape(N_SECTION, N_REP * MB, TOK_MB, D), sums)
```

```python
import jax
import jax.numpy as jnp
from jax import lax
from jax.experimental import pallas as pl
from jax.experimental.pallas import tpu as pltpu
from jax.sharding import PartitionSpec as P

EPSILON = 1e-05
HALF_ROOT = 0.7071067811865476
DENSITY = 0.3989422804014327
MESH = pl.DeviceIdType.MESH

D = 9216
R = 256
TOK = 64
ROWS = 128
NSEC = 8
NZ = 8
QUAD = D // NZ
SHARD = QUAD // 4
HALF = SHARD // 2
BLK = 16
NBLK = ROWS // BLK
NCH = 4
CHW = D // NCH
QPC = NZ // NCH
ECH = 8
ECW = D // ECH
NSEM = 160
F32 = jnp.float32
BF16 = jnp.bfloat16


def nn(left, right):
    return lax.dot_general(left, right, (((1,), (0,)), ((), ())), preferred_element_type=F32)


def nt(left, right):
    return lax.dot_general(left, right, (((1,), (1,)), ((), ())), preferred_element_type=F32)


def tn(left, right):
    return lax.dot_general(left, right, (((0,), (0,)), ((), ())), preferred_element_type=F32)


def kernel(
    hist_h, codes_h, scales, ids, cot_h, gain, bias, wd_h, wu_h,
    ig_h, ag_h,
    hist, codes, xin, norm, wd, wu, grad, res,
    acc, slopes, qmat, ugain, hidden, acts, mean_s, inv_s, scol,
    pd, pu, qd, qu, xsend, xrecv, su, ru, sd, rd, usend, urecv, final,
    ss, rs, css, crs, osem, lsem,
):
    sec = lax.axis_index("section")
    rep = lax.axis_index("rep")
    z = rep // 4
    xl = (rep // 2) % 2
    core = rep % 2
    oxl = 1 - xl
    ocore = 1 - core

    def zi(step):
        return (z + step + NZ) % NZ

    def at_z(step):
        return (sec, zi(step) * 4 + xl * 2 + core)

    up, down = at_z(1), at_z(-1)
    side = (sec, z * 4 + oxl * 2 + core)
    twin = (sec, z * 4 + xl * 2 + ocore)
    below = (jnp.maximum(sec - 1, 0), rep)
    above = (jnp.minimum(sec + 1, NSEC - 1), rep)

    names = {}
    pending = []

    def sid(name):
        return names.setdefault(name, len(names))

    def link(name, src, dst, device):
        index = sid(name)
        return pltpu.make_async_remote_copy(
            src_ref=src, dst_ref=dst, send_sem=ss.at[index], recv_sem=rs.at[index],
            device_id=device, device_id_type=MESH,
        )

    def put(name, src, dst, device):
        copy = link(name, src, dst, device)
        copy.start()
        pending.append(copy)

    def got(name, dst, device):
        link(name, dst, dst, device).wait_recv()

    loads = [
        pltpu.make_async_copy(hist_h.at[0], hist, lsem.at[0]),
        pltpu.make_async_copy(codes_h.at[0], codes, lsem.at[1]),
        pltpu.make_async_copy(wd_h.at[0], wd.at[z, xl, core], lsem.at[2]),
        pltpu.make_async_copy(wu_h.at[0], wu.at[z, xl, core], lsem.at[3]),
    ]
    for load in loads:
        load.start()

    def seed(m):
        return pltpu.make_async_copy(cot_h.at[m], grad.at[pl.ds(m * TOK, TOK)], lsem.at[4 + m])

    @pl.when(sec == NSEC - 1)
    def _():
        for m in range(2):
            seed(m).start()

    barrier = pltpu.get_barrier_semaphore()
    for device in (up, down, side, twin):
        pl.semaphore_signal(barrier, inc=1, device_id=device, device_id_type=MESH)

    @pl.when(sec > 0)
    def _():
        pl.semaphore_signal(barrier, inc=1, device_id=below, device_id_type=MESH)

    @pl.when(sec < NSEC - 1)
    def _():
        pl.semaphore_signal(barrier, inc=1, device_id=above, device_id_type=MESH)

    @pl.when((sec > 0) & (sec < NSEC - 1))
    def _():
        pl.semaphore_wait(barrier, 6)

    @pl.when((sec == 0) | (sec == NSEC - 1))
    def _():
        pl.semaphore_wait(barrier, 5)

    own_d, own_u = wd.at[z, xl, core], wu.at[z, xl, core]
    put("Ux0", wu_h.at[0], own_u, side)
    put("Dz+0", wd_h.at[0], own_d, up)
    put("Dz-0", wd_h.at[0], own_d, down)
    put("Uz+0s", wu_h.at[0], own_u, up)
    put("Uz-0s", wu_h.at[0], own_u, down)
    put("Dx0", wd_h.at[0], own_d, side)
    put("Ds0", wd_h.at[0], own_d, twin)
    put("Us0", wu_h.at[0], own_u, twin)

    for load in loads[:2]:
        load.wait()

    eye = (
        lax.broadcasted_iota(jnp.int32, (TOK, TOK), 0)
        == lax.broadcasted_iota(jnp.int32, (TOK, TOK), 1)
    )
    for m in range(2):
        row = scales[0, pl.ds(m, 1), :]
        scol[pl.ds(m * TOK, TOK), :] = jnp.sum(
            jnp.where(eye, row, 0.0), axis=1, keepdims=True
        )

    def rebuild(i):
        rows = pl.ds(pl.multiple_of(i * BLK, BLK), BLK)
        m = i // (TOK // BLK)
        inner = pl.ds(pl.multiple_of((i % (TOK // BLK)) * BLK, BLK), BLK)
        step = scol[rows, :]
        pick = ids[0, m]
        total = jnp.zeros((BLK, 1), F32)
        for e in range(ECH):
            cols = pl.ds(e * ECW, ECW)
            value = hist[pick, inner, cols].astype(F32) + step * codes[m, inner, cols].astype(F32)
            value = value.astype(BF16)
            xin[rows, cols] = value
            total = total + jnp.sum(value.astype(F32), axis=1, keepdims=True)
        mean = total * (1.0 / D)
        square = jnp.zeros((BLK, 1), F32)
        for e in range(ECH):
            cols = pl.ds(e * ECW, ECW)
            centred = xin[rows, cols].astype(F32) - mean
            square = square + jnp.sum(centred * centred, axis=1, keepdims=True)
        inv = lax.rsqrt(square * (1.0 / D) + EPSILON)
        mean_s[rows, :] = mean
        inv_s[rows, :] = inv
        for e in range(ECH):
            cols = pl.ds(e * ECW, ECW)
            scaled = (xin[rows, cols].astype(F32) - mean) * inv
            norm[rows, cols] = (scaled * gain[:, cols] + bias[:, cols]).astype(BF16)

    def rebuild_some(first, count):
        def step(i, carry):
            rebuild(first + i)
            return carry

        lax.fori_loop(0, count, step, 0)

    def extra_rows():
        line = lax.broadcasted_iota(jnp.int32, (BLK, ECW), 0)
        for e in range(ECH):
            cols = pl.ds(e * ECW, ECW)
            g, b = gain[:, cols], bias[:, cols]
            g_hi, b_hi = g.astype(BF16).astype(F32), b.astype(BF16).astype(F32)
            stack = jnp.where(line == 0, g_hi, 0.0)
            stack = jnp.where(line == 1, g - g_hi, stack)
            stack = jnp.where(line == 2, b_hi, stack)
            stack = jnp.where(line == 3, b - b_hi, stack)
            norm[pl.ds(ROWS, BLK), cols] = stack.astype(BF16)

    def quad_cols(q):
        return pl.ds(pl.multiple_of(q * QUAD, QUAD), QUAD)

    def forward(q, first=False):
        part = nn(norm[:, quad_cols(q)], wd[q].reshape(QUAD, R))
        if first:
            acc[...] = part
        else:
            acc[...] += part

    extra_rows()
    got("Ux0", wu.at[z, oxl, core], side)
    put("Uz+0p", wu.at[z, oxl, core], wu.at[z, oxl, core], up)
    put("Uz-0p", wu.at[z, oxl, core], wu.at[z, oxl, core], down)
    put("Uxs0", wu.at[z, oxl, core], wu.at[z, oxl, core], twin)
    got("Dx0", wd.at[z, oxl, core], side)
    put("Dxs0", wd.at[z, oxl, core], wd.at[z, oxl, core], twin)
    rebuild_some(0, 2)

    def piece(ref, direction, dist, e, c):
        q = zi(-dist if direction == "+" else dist)
        if dist < 4 or ref is wu:
            return ref.at[q, e, c]
        first = 0 if direction == "+" else HALF
        return ref.at[q, e, c, pl.ds(first, HALF)]

    def onward(ref, direction, dist, e, c):
        q = zi(-dist if direction == "+" else dist)
        if dist < 3 or ref is wu:
            return ref.at[q, e, c]
        first = 0 if direction == "+" else HALF
        return ref.at[q, e, c, pl.ds(first, HALF)]

    ways = (("+", up, down), ("-", down, up))

    def down_ready(dist):
        if dist == 0:
            got("Ds0", wd.at[z, xl, ocore], twin)
            got("Dxs0", wd.at[z, oxl, ocore], twin)
            return
        for way, _, _ in ways:
            got(f"Ds{way}{dist}", piece(wd, way, dist, xl, ocore), twin)
            got(f"Dxs{way}{dist}", piece(wd, way, dist, oxl, ocore), twin)

    for dist in range(1, 5):
        for way, ahead, behind in ways:
            part = piece(wd, way, dist, xl, core)
            got(f"Dz{way}{dist - 1}", part, behind)
            if dist < 4:
                more = onward(wd, way, dist, xl, core)
                put(f"Dz{way}{dist}", more, more, ahead)
            put(f"Dx{way}{dist}", part, part, side)
            put(f"Ds{way}{dist}", part, part, twin)
        for which, e in (("s", xl), ("p", oxl)):
            for way, ahead, behind in ways:
                if dist == 4 and (way == "+") != (which == "s"):
                    continue
                part = piece(wu, way, dist, e, core)
                got(f"Uz{way}{dist - 1}{which}", part, behind)
                if dist < 3 or (dist == 3 and (way == "+") == (which == "s")):
                    put(f"Uz{way}{dist}{which}", part, part, ahead)
                put(f"Us{way}{dist}{which}", part, part, twin)
        for way, ahead, behind in ways:
            part = piece(wd, way, dist, oxl, core)
            got(f"Dx{way}{dist}", part, side)
            put(f"Dxs{way}{dist}", part, part, twin)
        if dist < 4:
            rebuild_some(2 * dist, 2)
        if dist == 3:
            loads[2].wait()
            down_ready(0)
            forward(zi(0), True)
            down_ready(1)
            forward(zi(-1))
            forward(zi(1))
    for dist in (2, 3):
        down_ready(dist)
        forward(zi(-dist))
        forward(zi(dist))
    down_ready(4)
    forward(zi(4))

    shift = acc[ROWS + 2 : ROWS + 3, :] + acc[ROWS + 3 : ROWS + 4, :]
    ugain[...] = acc[ROWS : ROWS + 1, :] + acc[ROWS + 1 : ROWS + 2, :]
    for i in range(4):
        rows = pl.ds(i * 32, 32)
        preact = acc[rows, :]
        cdf = 0.5 * (1.0 + lax.erf(preact * HALF_ROOT))
        bump = DENSITY * jnp.exp(-0.5 * preact * preact)
        hidden[rows, :] = (preact * cdf).astype(BF16)
        slopes[rows, :] = cdf + preact * bump
        qmat[rows, :] = preact - shift

    loads[3].wait()
    got("Us0", wu.at[z, xl, ocore], twin)
    got("Uxs0", wu.at[z, oxl, ocore], twin)
    for dist in range(1, 5):
        for which, e in (("s", xl), ("p", oxl)):
            for way, _, _ in ways:
                if dist == 4 and (way == "+") != (which == "s"):
                    continue
                got(f"Us{way}{dist}{which}", piece(wu, way, dist, e, ocore), twin)

    @pl.when(sec == NSEC - 1)
    def _():
        for m in range(2):
            seed(m).wait()

    def hop(i, ch, src):
        rows = pl.ds(pl.multiple_of(i * BLK, BLK), BLK)
        index = i * NCH + ch
        return pltpu.make_async_remote_copy(
            src_ref=src.at[rows, pl.ds(ch * CHW, CHW)],
            dst_ref=grad.at[rows, pl.ds(ch * CHW, CHW)],
            send_sem=css.at[index], recv_sem=crs.at[index],
            device_id=below, device_id_type=MESH,
        )

    def keep(i):
        inner = pl.ds(pl.multiple_of((i % (TOK // BLK)) * BLK, BLK), BLK)
        rows = pl.ds(pl.multiple_of(i * BLK, BLK), BLK)
        return pltpu.make_async_copy(
            res.at[rows], ig_h.at[0, i // (TOK // BLK), inner], osem.at[i]
        )

    def chain(i, carry):
        rows = pl.ds(pl.multiple_of(i * BLK, BLK), BLK)
        lift = jnp.zeros((BLK, R), F32)
        for ch in range(NCH):
            @pl.when(sec < NSEC - 1)
            def _():
                hop(i, ch, grad).wait_recv()

            lift = lift + nn(
                grad[rows, ch * CHW : (ch + 1) * CHW],
                wu[ch * QPC : (ch + 1) * QPC].reshape(CHW, R),
            )
        act = (lift * slopes[rows, :]).astype(BF16)
        acts[rows, :] = act
        wide = act.astype(F32)
        m1 = jnp.sum(wide * ugain[...], axis=1, keepdims=True) * (1.0 / D)
        m2 = jnp.sum(wide * qmat[rows, :], axis=1, keepdims=True) * (1.0 / D)
        mean, inv = mean_s[rows, :], inv_s[rows, :]
        tilt = inv * inv * m2
        base = inv * m1 - mean * tilt
        for ch in range(NCH):
            cols = pl.ds(ch * CHW, CHW)
            back = nt(act, wd[ch * QPC : (ch + 1) * QPC].reshape(CHW, R))
            value = (
                grad[rows, cols].astype(F32) + inv * (back * gain[:, cols]) - base
                - xin[rows, cols].astype(F32) * tilt
            )
            res[rows, cols] = value.astype(BF16)

            @pl.when(sec > 0)
            def _():
                hop(i, ch, res).start()

        keep(i).start()
        return carry

    lax.fori_loop(0, NBLK, chain, 0)

    def terms(q):
        cols = quad_cols(q)
        pd[q] = (tn(norm[:ROWS, cols], acts[...]) * (1.0 / TOK)).astype(BF16).reshape(2, 2, SHARD, R)
        pu[q] = (tn(grad[:, cols], hidden[...]) * (1.0 / TOK)).astype(BF16).reshape(2, 2, SHARD, R)

    def make(step):
        q = zi(step)
        terms(q)
        put(f"Pu{step}", pu.at[q, :, ocore], qu.at[q], twin)
        put(f"Pd{step}", pd.at[q, :, ocore], qd.at[q], twin)

    def heard(step):
        q = zi(step)
        got(f"Pu{step}", qu.at[q], twin)
        got(f"Pd{step}", qd.at[q], twin)

    def cross(step):
        q = zi(step)
        xsend[q] = (pd[q, oxl, core].astype(F32) + qd[q, oxl].astype(F32)).astype(BF16)
        put(f"X{step}", xsend.at[q], xrecv.at[q], side)

    def send_up_half(j):
        dist = 4 - j
        for way, ahead, behind in ways:
            d = 0 if way == "+" else 1
            q = zi(dist if way == "+" else -dist)
            order = ("p", "s") if way == "+" else ("s", "p")
            for which in order:
                lead = (way == "+") == (which == "s")
                if j == 0 and not lead:
                    continue
                e, k = (xl, 0) if which == "s" else (oxl, 1)
                value = pu[q, e, core].astype(F32) + qu[q, e].astype(F32)
                if j >= 2 or (j == 1 and lead):
                    got(f"RU{way}{j - 1}{which}", ru.at[d, j - 1, k], behind)
                    value = value + ru[d, j - 1, k].astype(F32)
                su[d, j, k] = value.astype(BF16)
                put(f"RU{way}{j}{which}", su.at[d, j, k], ru.at[d, j, k], ahead)

    def send_down_half(j):
        dist = 4 - j
        if j == 0:
            got("X4", xrecv.at[zi(4)], side)
        else:
            for way, _, _ in ways:
                step = dist if way == "+" else -dist
                got(f"X{step}", xrecv.at[zi(step)], side)
        for way, ahead, behind in ways:
            d = 0 if way == "+" else 1
            q = zi(dist if way == "+" else -dist)
            part = pl.ds(0 if way == "+" else HALF, HALF)
            if j == 0:
                value = (
                    pd[q, xl, core, part].astype(F32) + qd[q, xl, part].astype(F32)
                    + xrecv[q, part].astype(F32)
                )
                sd[d, 0, part] = value.astype(BF16)
                put(f"RD{way}0", sd.at[d, 0, part], rd.at[d, 0, part], ahead)
                continue
            value = (
                pd[q, xl, core].astype(F32) + qd[q, xl].astype(F32) + xrecv[q].astype(F32)
            )
            sd[d, j] = value.astype(BF16)
            if j == 1:
                got(f"RD{way}0", rd.at[d, 0, part], behind)
                sd[d, j, part] = (
                    pd[q, xl, core, part].astype(F32) + qd[q, xl, part].astype(F32)
                    + xrecv[q, part].astype(F32) + rd[d, 0, part].astype(F32)
                ).astype(BF16)
            else:
                got(f"RD{way}{j - 1}", rd.at[d, j - 1], behind)
                sd[d, j] = (value + rd[d, j - 1].astype(F32)).astype(BF16)
            put(f"RD{way}{j}", sd.at[d, j], rd.at[d, j], ahead)

    make(4)
    make(3)
    make(-3)
    heard(4)
    send_up_half(0)
    cross(4)
    make(2)
    make(-2)
    heard(3)
    heard(-3)
    send_up_half(1)
    cross(3)
    cross(-3)
    make(1)
    make(-1)
    send_down_half(0)
    make(0)
    heard(2)
    heard(-2)
    send_up_half(2)
    cross(2)
    cross(-2)
    heard(1)
    heard(-1)
    cross(1)
    cross(-1)
    heard(0)
    cross(0)
    send_down_half(1)
    send_up_half(3)
    send_down_half(2)
    for way, _, behind in ways:
        d = 0 if way == "+" else 1
        got(f"RU{way}3p", ru.at[d, 3, 1], behind)
    usend[...] = (
        pu[z, oxl, core].astype(F32) + qu[z, oxl].astype(F32)
        + ru[0, 3, 1].astype(F32) + ru[1, 3, 1].astype(F32)
    ).astype(BF16)
    put("UF", usend, urecv, side)
    send_down_half(3)
    for way, _, behind in ways:
        d = 0 if way == "+" else 1
        got(f"RU{way}3s", ru.at[d, 3, 0], behind)
    got("UF", urecv, side)
    final[:, pl.ds(R, R)] = (
        pu[z, xl, core].astype(F32) + qu[z, xl].astype(F32)
        + ru[0, 3, 0].astype(F32) + ru[1, 3, 0].astype(F32) + urecv[...].astype(F32)
    )
    got("X0", xrecv.at[z], side)
    for way, _, behind in ways:
        d = 0 if way == "+" else 1
        got(f"RD{way}3", rd.at[d, 3], behind)
    final[:, pl.ds(0, R)] = (
        pd[z, xl, core].astype(F32) + qd[z, xl].astype(F32) + xrecv[z].astype(F32)
        + rd[0, 3].astype(F32) + rd[1, 3].astype(F32)
    )
    store = pltpu.make_async_copy(final, ag_h.at[0], lsem.at[6])
    store.start()

    for copy in pending:
        copy.wait_send()

    def settle(i, carry):
        @pl.when(sec > 0)
        def _():
            for ch in range(NCH):
                hop(i, ch, res).wait_send()

        keep(i).wait()
        return carry

    lax.fori_loop(0, NBLK, settle, 0)
    store.wait()
    assert len(names) <= NSEM


def per_device(*arrays):
    vmem = pl.BlockSpec(memory_space=pltpu.VMEM)
    smem = pl.BlockSpec(memory_space=pltpu.SMEM)
    hbm = pl.BlockSpec(memory_space=pl.ANY)
    return pl.pallas_call(
        kernel,
        out_shape=(
            jax.ShapeDtypeStruct((1, 2, TOK, D), BF16),
            jax.ShapeDtypeStruct((1, SHARD, 2 * R), F32),
        ),
        in_specs=[hbm, hbm, vmem, smem, hbm, vmem, vmem, hbm, hbm],
        out_specs=(hbm, hbm),
        scratch_shapes=[
            pltpu.VMEM((2, TOK, D), BF16),
            pltpu.VMEM((2, TOK, D), jnp.int32),
            pltpu.VMEM((ROWS, D), BF16),
            pltpu.VMEM((ROWS + BLK, D), BF16),
            pltpu.VMEM((NZ, 2, 2, SHARD, R), BF16),
            pltpu.VMEM((NZ, 2, 2, SHARD, R), BF16),
            pltpu.VMEM((ROWS, D), BF16),
            pltpu.VMEM((ROWS, D), BF16),
            pltpu.VMEM((ROWS + BLK, R), F32),
            pltpu.VMEM((ROWS, R), F32),
            pltpu.VMEM((ROWS, R), F32),
            pltpu.VMEM((1, R), F32),
            pltpu.VMEM((ROWS, R), BF16),
            pltpu.VMEM((ROWS, R), BF16),
            pltpu.VMEM((ROWS, 1), F32),
            pltpu.VMEM((ROWS, 1), F32),
            pltpu.VMEM((ROWS, 1), F32),
            pltpu.VMEM((NZ, 2, 2, SHARD, R), BF16),
            pltpu.VMEM((NZ, 2, 2, SHARD, R), BF16),
            pltpu.VMEM((NZ, 2, SHARD, R), BF16),
            pltpu.VMEM((NZ, 2, SHARD, R), BF16),
            pltpu.VMEM((NZ, SHARD, R), BF16),
            pltpu.VMEM((NZ, SHARD, R), BF16),
            pltpu.VMEM((2, 4, 2, SHARD, R), BF16),
            pltpu.VMEM((2, 4, 2, SHARD, R), BF16),
            pltpu.VMEM((2, 4, SHARD, R), BF16),
            pltpu.VMEM((2, 4, SHARD, R), BF16),
            pltpu.VMEM((SHARD, R), BF16),
            pltpu.VMEM((SHARD, R), BF16),
            pltpu.VMEM((SHARD, 2 * R), F32),
            pltpu.SemaphoreType.DMA((NSEM,)),
            pltpu.SemaphoreType.DMA((NSEM,)),
            pltpu.SemaphoreType.DMA((NBLK * NCH,)),
            pltpu.SemaphoreType.DMA((NBLK * NCH,)),
            pltpu.SemaphoreType.DMA((NBLK,)),
            pltpu.SemaphoreType.DMA((8,)),
        ],
        compiler_params=pltpu.CompilerParams(
            collective_id=0, has_side_effects=True, vmem_limit_bytes=60 << 20
        ),
        cost_estimate=pl.CostEstimate(
            flops=10 * ROWS * D * R, bytes_accessed=24 << 20, transcendentals=2 * ROWS * R
        ),
    )(*arrays)


def solution(mesh):
    return jax.shard_map(
        per_device,
        mesh=mesh,
        in_specs=(
            P("section", "rep", None, None),
            P("section", "rep", None, None),
            P("section", "rep", None),
            P("rep", None),
            P("rep", None, None),
            P("section", None),
            P("section", None),
            P("section", "rep", None),
            P("section", "rep", None),
        ),
        out_specs=(P("section", "rep", None, None), P("section", "rep", None)),
        check_vma=False,
    )
```

```python
import jax
import jax.numpy as jnp
from jax import lax
from jax.experimental import pallas as pl
from jax.experimental.pallas import tpu as pltpu
from jax.sharding import PartitionSpec as P

EPSILON = 1e-05
HALF_ROOT = 0.7071067811865476
DENSITY = 0.3989422804014327
MESH = pl.DeviceIdType.MESH

D = 9216
R = 256
TOK = 64
ROWS = 128
NSEC = 8
NZ = 8
QUAD = D // NZ
SHARD = QUAD // 4
HALF = SHARD // 2
BLK = 16
NBLK = ROWS // BLK
ECH = 8
ECW = D // ECH
NSEM = 96
F32 = jnp.float32
BF16 = jnp.bfloat16


def nn(left, right):
    return lax.dot_general(left, right, (((1,), (0,)), ((), ())), preferred_element_type=F32)


def nt(left, right):
    return lax.dot_general(left, right, (((1,), (1,)), ((), ())), preferred_element_type=F32)


def tn(left, right):
    return lax.dot_general(left, right, (((0,), (0,)), ((), ())), preferred_element_type=F32)


def kernel(
    hist_h, codes_h, scales, ids, cot_h, gain, bias, wd_h, wu_h,
    ig_h, ag_h,
    hist, codes, xin, norm, wd, wu, grad, res,
    acc, slopes, qmat, ugain, hidden, acts, mean_s, inv_s, scol,
    gather_n, gather_g, gather_h, gather_a, total, tsend, trecv, xsend, xrecv, final,
    ss, rs, css, crs, gss, grs, ass, ars, osem, lsem,
):
    sec = lax.axis_index("section")
    rep = lax.axis_index("rep")
    z = rep // 4
    xl = (rep // 2) % 2
    core = rep % 2
    oxl = 1 - xl
    ocore = 1 - core

    def zi(step):
        return (z + step + NZ) % NZ

    def at_z(step):
        return (sec, zi(step) * 4 + xl * 2 + core)

    up, down = at_z(1), at_z(-1)
    side = (sec, z * 4 + oxl * 2 + core)
    twin = (sec, z * 4 + xl * 2 + ocore)
    below = (jnp.maximum(sec - 1, 0), rep)
    above = (jnp.minimum(sec + 1, NSEC - 1), rep)

    names = {}
    pending = []

    def sid(name):
        return names.setdefault(name, len(names))

    def link(name, src, dst, device):
        index = sid(name)
        return pltpu.make_async_remote_copy(
            src_ref=src, dst_ref=dst, send_sem=ss.at[index], recv_sem=rs.at[index],
            device_id=device, device_id_type=MESH,
        )

    def put(name, src, dst, device):
        copy = link(name, src, dst, device)
        copy.start()
        pending.append(copy)

    def got(name, dst, device):
        link(name, dst, dst, device).wait_recv()

    loads = [
        pltpu.make_async_copy(hist_h.at[0], hist, lsem.at[0]),
        pltpu.make_async_copy(codes_h.at[0], codes, lsem.at[1]),
        pltpu.make_async_copy(wd_h.at[0], wd.at[z, xl, core], lsem.at[2]),
        pltpu.make_async_copy(wu_h.at[0], wu.at[z, xl, core], lsem.at[3]),
    ]
    for load in loads:
        load.start()

    def seed(m):
        return pltpu.make_async_copy(cot_h.at[m], grad.at[pl.ds(m * TOK, TOK)], lsem.at[4 + m])

    @pl.when(sec == NSEC - 1)
    def _():
        for m in range(2):
            seed(m).start()

    barrier = pltpu.get_barrier_semaphore()
    ring = [at_z(step) for step in range(1, NZ)]
    for device in (*ring, side, twin):
        pl.semaphore_signal(barrier, inc=1, device_id=device, device_id_type=MESH)

    @pl.when(sec > 0)
    def _():
        pl.semaphore_signal(barrier, inc=1, device_id=below, device_id_type=MESH)

    @pl.when(sec < NSEC - 1)
    def _():
        pl.semaphore_signal(barrier, inc=1, device_id=above, device_id_type=MESH)

    @pl.when((sec > 0) & (sec < NSEC - 1))
    def _():
        pl.semaphore_wait(barrier, len(ring) + 4)

    @pl.when((sec == 0) | (sec == NSEC - 1))
    def _():
        pl.semaphore_wait(barrier, len(ring) + 3)

    own_d, own_u = wd.at[z, xl, core], wu.at[z, xl, core]
    put("Ux0", wu_h.at[0], own_u, side)
    put("Dz+0", wd_h.at[0], own_d, up)
    put("Dz-0", wd_h.at[0], own_d, down)
    put("Uz+0s", wu_h.at[0], own_u, up)
    put("Uz-0s", wu_h.at[0], own_u, down)
    put("Dx0", wd_h.at[0], own_d, side)
    put("Ds0", wd_h.at[0], own_d, twin)
    put("Us0", wu_h.at[0], own_u, twin)

    for load in loads[:2]:
        load.wait()

    eye = (
        lax.broadcasted_iota(jnp.int32, (TOK, TOK), 0)
        == lax.broadcasted_iota(jnp.int32, (TOK, TOK), 1)
    )
    for m in range(2):
        row = scales[0, pl.ds(m, 1), :]
        scol[pl.ds(m * TOK, TOK), :] = jnp.sum(
            jnp.where(eye, row, 0.0), axis=1, keepdims=True
        )

    def rebuild(i):
        rows = pl.ds(pl.multiple_of(i * BLK, BLK), BLK)
        m = i // (TOK // BLK)
        inner = pl.ds(pl.multiple_of((i % (TOK // BLK)) * BLK, BLK), BLK)
        step = scol[rows, :]
        pick = ids[0, m]
        total = jnp.zeros((BLK, 1), F32)
        for e in range(ECH):
            cols = pl.ds(e * ECW, ECW)
            value = hist[pick, inner, cols].astype(F32) + step * codes[m, inner, cols].astype(F32)
            value = value.astype(BF16)
            xin[rows, cols] = value
            total = total + jnp.sum(value.astype(F32), axis=1, keepdims=True)
        mean = total * (1.0 / D)
        square = jnp.zeros((BLK, 1), F32)
        for e in range(ECH):
            cols = pl.ds(e * ECW, ECW)
            centred = xin[rows, cols].astype(F32) - mean
            square = square + jnp.sum(centred * centred, axis=1, keepdims=True)
        inv = lax.rsqrt(square * (1.0 / D) + EPSILON)
        mean_s[rows, :] = mean
        inv_s[rows, :] = inv
        for e in range(ECH):
            cols = pl.ds(e * ECW, ECW)
            scaled = (xin[rows, cols].astype(F32) - mean) * inv
            norm[rows, cols] = (scaled * gain[:, cols] + bias[:, cols]).astype(BF16)

    def rebuild_some(first, count):
        def step(i, carry):
            rebuild(first + i)
            return carry

        lax.fori_loop(0, count, step, 0)

    def extra_rows():
        line = lax.broadcasted_iota(jnp.int32, (BLK, ECW), 0)
        for e in range(ECH):
            cols = pl.ds(e * ECW, ECW)
            g, b = gain[:, cols], bias[:, cols]
            g_hi, b_hi = g.astype(BF16).astype(F32), b.astype(BF16).astype(F32)
            stack = jnp.where(line == 0, g_hi, 0.0)
            stack = jnp.where(line == 1, g - g_hi, stack)
            stack = jnp.where(line == 2, b_hi, stack)
            stack = jnp.where(line == 3, b - b_hi, stack)
            norm[pl.ds(ROWS, BLK), cols] = stack.astype(BF16)

    def quad_cols(q):
        return pl.ds(pl.multiple_of(q * QUAD, QUAD), QUAD)

    def forward(q, first=False):
        part = nn(norm[:, quad_cols(q)], wd[q].reshape(QUAD, R))
        if first:
            acc[...] = part
        else:
            acc[...] += part

    extra_rows()
    got("Ux0", wu.at[z, oxl, core], side)
    put("Uz+0p", wu.at[z, oxl, core], wu.at[z, oxl, core], up)
    put("Uz-0p", wu.at[z, oxl, core], wu.at[z, oxl, core], down)
    put("Uxs0", wu.at[z, oxl, core], wu.at[z, oxl, core], twin)
    got("Dx0", wd.at[z, oxl, core], side)
    put("Dxs0", wd.at[z, oxl, core], wd.at[z, oxl, core], twin)
    rebuild_some(0, 2)

    def piece(ref, direction, dist, e, c):
        q = zi(-dist if direction == "+" else dist)
        if dist < 4 or ref is wu:
            return ref.at[q, e, c]
        first = 0 if direction == "+" else HALF
        return ref.at[q, e, c, pl.ds(first, HALF)]

    def onward(ref, direction, dist, e, c):
        q = zi(-dist if direction == "+" else dist)
        if dist < 3 or ref is wu:
            return ref.at[q, e, c]
        first = 0 if direction == "+" else HALF
        return ref.at[q, e, c, pl.ds(first, HALF)]

    ways = (("+", up, down), ("-", down, up))

    def down_ready(dist):
        if dist == 0:
            got("Ds0", wd.at[z, xl, ocore], twin)
            got("Dxs0", wd.at[z, oxl, ocore], twin)
            return
        for way, _, _ in ways:
            got(f"Ds{way}{dist}", piece(wd, way, dist, xl, ocore), twin)
            got(f"Dxs{way}{dist}", piece(wd, way, dist, oxl, ocore), twin)

    for dist in range(1, 5):
        for way, ahead, behind in ways:
            part = piece(wd, way, dist, xl, core)
            got(f"Dz{way}{dist - 1}", part, behind)
            if dist < 4:
                more = onward(wd, way, dist, xl, core)
                put(f"Dz{way}{dist}", more, more, ahead)
            put(f"Dx{way}{dist}", part, part, side)
            put(f"Ds{way}{dist}", part, part, twin)
        for which, e in (("s", xl), ("p", oxl)):
            for way, ahead, behind in ways:
                if dist == 4 and (way == "+") != (which == "s"):
                    continue
                part = piece(wu, way, dist, e, core)
                got(f"Uz{way}{dist - 1}{which}", part, behind)
                if dist < 3 or (dist == 3 and (way == "+") == (which == "s")):
                    put(f"Uz{way}{dist}{which}", part, part, ahead)
                put(f"Us{way}{dist}{which}", part, part, twin)
        for way, ahead, behind in ways:
            part = piece(wd, way, dist, oxl, core)
            got(f"Dx{way}{dist}", part, side)
            put(f"Dxs{way}{dist}", part, part, twin)
        if dist < 4:
            rebuild_some(2 * dist, 2)
        if dist == 3:
            loads[2].wait()
            down_ready(0)
            forward(zi(0), True)
            down_ready(1)
            forward(zi(-1))
            forward(zi(1))
    for dist in (2, 3):
        down_ready(dist)
        forward(zi(-dist))
        forward(zi(dist))
    down_ready(4)
    forward(zi(4))

    shift = acc[ROWS + 2 : ROWS + 3, :] + acc[ROWS + 3 : ROWS + 4, :]
    ugain[...] = acc[ROWS : ROWS + 1, :] + acc[ROWS + 1 : ROWS + 2, :]
    for i in range(4):
        rows = pl.ds(i * 32, 32)
        preact = acc[rows, :]
        cdf = 0.5 * (1.0 + lax.erf(preact * HALF_ROOT))
        bump = DENSITY * jnp.exp(-0.5 * preact * preact)
        hidden[rows, :] = (preact * cdf).astype(BF16)
        slopes[rows, :] = cdf + preact * bump
        qmat[rows, :] = preact - shift

    loads[3].wait()
    got("Us0", wu.at[z, xl, ocore], twin)
    got("Uxs0", wu.at[z, oxl, ocore], twin)
    for dist in range(1, 5):
        for which, e in (("s", xl), ("p", oxl)):
            for way, _, _ in ways:
                if dist == 4 and (way == "+") != (which == "s"):
                    continue
                got(f"Us{way}{dist}{which}", piece(wu, way, dist, e, ocore), twin)

    @pl.when(sec == NSEC - 1)
    def _():
        for m in range(2):
            seed(m).wait()

    for step in range(1, NZ):
        q = zi(step)
        put(f"N{step}", norm.at[pl.ds(0, ROWS), quad_cols(q)], gather_n.at[z], at_z(step))
    own_n = pltpu.make_async_copy(
        norm.at[pl.ds(0, ROWS), quad_cols(z)], gather_n.at[z], lsem.at[7]
    )
    own_n.start()
    for step in range(1, NZ):
        put(f"H{step}", hidden, gather_h.at[z], at_z(step))
    gather_h[z] = hidden[...]

    def rows_of(i):
        return pl.ds(pl.multiple_of(i * BLK, BLK), BLK)

    def hop(i, n, src):
        part = (rows_of(i), quad_cols(zi(n + 1)))
        index = i * NZ + n
        return pltpu.make_async_remote_copy(
            src_ref=src.at[part], dst_ref=grad.at[part],
            send_sem=css.at[index], recv_sem=crs.at[index],
            device_id=below, device_id_type=MESH,
        )

    def spread_grad(i, n, landing):
        index = i * NZ + n
        return pltpu.make_async_remote_copy(
            src_ref=grad.at[rows_of(i), quad_cols(zi(n + 1))],
            dst_ref=gather_g.at[landing, rows_of(i)],
            send_sem=gss.at[index], recv_sem=grs.at[index],
            device_id=at_z(n + 1), device_id_type=MESH,
        )

    def own_grad(i):
        return pltpu.make_async_copy(
            grad.at[rows_of(i), quad_cols(z)], gather_g.at[z, rows_of(i)],
            grs.at[i * NZ + NZ - 1],
        )

    def spread_act(i, n, landing):
        index = i * NZ + n
        return pltpu.make_async_remote_copy(
            src_ref=acts.at[rows_of(i)], dst_ref=gather_a.at[landing, rows_of(i)],
            send_sem=ass.at[index], recv_sem=ars.at[index],
            device_id=at_z(n + 1), device_id_type=MESH,
        )

    def keep(i):
        inner = pl.ds(pl.multiple_of((i % (TOK // BLK)) * BLK, BLK), BLK)
        return pltpu.make_async_copy(
            res.at[rows_of(i)], ig_h.at[0, i // (TOK // BLK), inner], osem.at[i]
        )

    def chain(i, carry):
        rows = rows_of(i)
        lift = jnp.zeros((BLK, R), F32)
        for n in range(NZ):
            q = zi(n + 1)

            @pl.when(sec < NSEC - 1)
            def _():
                hop(i, n, grad).wait_recv()

            if n < NZ - 1:
                spread_grad(i, n, z).start()
            else:
                own_grad(i).start()
            lift = lift + nn(grad[rows, quad_cols(q)], wu[q].reshape(QUAD, R))
        act = (lift * slopes[rows, :]).astype(BF16)
        acts[rows, :] = act
        gather_a[z, rows, :] = act
        wide = act.astype(F32)
        m1 = jnp.sum(wide * ugain[...], axis=1, keepdims=True) * (1.0 / D)
        m2 = jnp.sum(wide * qmat[rows, :], axis=1, keepdims=True) * (1.0 / D)
        mean, inv = mean_s[rows, :], inv_s[rows, :]
        tilt = inv * inv * m2
        base = inv * m1 - mean * tilt
        for n in range(NZ):
            q = zi(n + 1)
            cols = quad_cols(q)
            back = nt(act, wd[q].reshape(QUAD, R))
            value = (
                grad[rows, cols].astype(F32) + inv * (back * gain[:, cols]) - base
                - xin[rows, cols].astype(F32) * tilt
            )
            res[rows, cols] = value.astype(BF16)

            @pl.when(sec > 0)
            def _():
                hop(i, n, res).start()

        for n in range(NZ - 1):
            spread_act(i, n, z).start()
        keep(i).start()
        return carry

    lax.fori_loop(0, NBLK, chain, 0)

    own_n.wait()
    for step in range(1, NZ):
        got(f"N{step}", gather_n.at[zi(-step)], at_z(-step))
        got(f"H{step}", gather_h.at[zi(-step)], at_z(-step))

    def arrived(i):
        for n in range(NZ - 1):
            spread_grad(i, n, zi(-(n + 1))).wait_recv()
            spread_act(i, n, zi(-(n + 1))).wait_recv()
        own_grad(i).wait()

    def add_terms(first, count, fresh):
        rows = pl.ds(first, count * BLK)
        depth = NZ * count * BLK
        for h, (wide_ref, thin_ref) in enumerate(((gather_n, gather_a), (gather_g, gather_h))):
            term = tn(
                wide_ref[:, rows, :].reshape(depth, QUAD), thin_ref[:, rows, :].reshape(depth, R)
            ).reshape(2, 2, SHARD, R)
            if fresh:
                total[h] = term
            else:
                total[h] += term

    first = 0
    for count in (2, 2, 2, 1, 1):
        for i in range(first, first + count):
            arrived(i)
        add_terms(first * BLK, count, first == 0)
        first += count

    scale = 1.0 / TOK
    for e in (oxl, xl):
        for h in range(2):
            tsend[h, e] = (total[h, e, ocore] * scale).astype(BF16)
            name = f"T{h}" + ("p" if e is oxl else "s")
            put(name, tsend.at[h, e], trecv.at[h, e], twin)
    for h in range(2):
        got(f"T{h}p", trecv.at[h, oxl], twin)
        xsend[h] = (total[h, oxl, core] * scale + trecv[h, oxl].astype(F32)).astype(BF16)
        put(f"X{h}", xsend.at[h], xrecv.at[h], side)
    for h in range(2):
        got(f"T{h}s", trecv.at[h, xl], twin)
        total[h, xl, core] = total[h, xl, core] * scale + trecv[h, xl].astype(F32)
    for h in range(2):
        got(f"X{h}", xrecv.at[h], side)
        final[:, pl.ds(h * R, R)] = total[h, xl, core] + xrecv[h].astype(F32)
    store = pltpu.make_async_copy(final, ag_h.at[0], lsem.at[6])
    store.start()

    for copy in pending:
        copy.wait_send()

    def settle(i, carry):
        @pl.when(sec > 0)
        def _():
            for n in range(NZ):
                hop(i, n, res).wait_send()

        for n in range(NZ - 1):
            spread_grad(i, n, z).wait_send()
            spread_act(i, n, z).wait_send()
        keep(i).wait()
        return carry

    lax.fori_loop(0, NBLK, settle, 0)
    store.wait()
    assert len(names) <= NSEM


def per_device(*arrays):
    vmem = pl.BlockSpec(memory_space=pltpu.VMEM)
    smem = pl.BlockSpec(memory_space=pltpu.SMEM)
    hbm = pl.BlockSpec(memory_space=pl.ANY)
    return pl.pallas_call(
        kernel,
        out_shape=(
            jax.ShapeDtypeStruct((1, 2, TOK, D), BF16),
            jax.ShapeDtypeStruct((1, SHARD, 2 * R), F32),
        ),
        in_specs=[hbm, hbm, vmem, smem, hbm, vmem, vmem, hbm, hbm],
        out_specs=(hbm, hbm),
        scratch_shapes=[
            pltpu.VMEM((2, TOK, D), BF16),
            pltpu.VMEM((2, TOK, D), jnp.int32),
            pltpu.VMEM((ROWS, D), BF16),
            pltpu.VMEM((ROWS + BLK, D), BF16),
            pltpu.VMEM((NZ, 2, 2, SHARD, R), BF16),
            pltpu.VMEM((NZ, 2, 2, SHARD, R), BF16),
            pltpu.VMEM((ROWS, D), BF16),
            pltpu.VMEM((ROWS, D), BF16),
            pltpu.VMEM((ROWS + BLK, R), F32),
            pltpu.VMEM((ROWS, R), F32),
            pltpu.VMEM((ROWS, R), F32),
            pltpu.VMEM((1, R), F32),
            pltpu.VMEM((ROWS, R), BF16),
            pltpu.VMEM((ROWS, R), BF16),
            pltpu.VMEM((ROWS, 1), F32),
            pltpu.VMEM((ROWS, 1), F32),
            pltpu.VMEM((ROWS, 1), F32),
            pltpu.VMEM((NZ, ROWS, QUAD), BF16),
            pltpu.VMEM((NZ, ROWS, QUAD), BF16),
            pltpu.VMEM((NZ, ROWS, R), BF16),
            pltpu.VMEM((NZ, ROWS, R), BF16),
            pltpu.VMEM((2, 2, 2, SHARD, R), F32),
            pltpu.VMEM((2, 2, SHARD, R), BF16),
            pltpu.VMEM((2, 2, SHARD, R), BF16),
            pltpu.VMEM((2, SHARD, R), BF16),
            pltpu.VMEM((2, SHARD, R), BF16),
            pltpu.VMEM((SHARD, 2 * R), F32),
            pltpu.SemaphoreType.DMA((NSEM,)),
            pltpu.SemaphoreType.DMA((NSEM,)),
            pltpu.SemaphoreType.DMA((NBLK * NZ,)),
            pltpu.SemaphoreType.DMA((NBLK * NZ,)),
            pltpu.SemaphoreType.DMA((NBLK * NZ,)),
            pltpu.SemaphoreType.DMA((NBLK * NZ,)),
            pltpu.SemaphoreType.DMA((NBLK * NZ,)),
            pltpu.SemaphoreType.DMA((NBLK * NZ,)),
            pltpu.SemaphoreType.DMA((NBLK,)),
            pltpu.SemaphoreType.DMA((8,)),
        ],
        compiler_params=pltpu.CompilerParams(
            collective_id=0, has_side_effects=True, vmem_limit_bytes=60 << 20
        ),
        cost_estimate=pl.CostEstimate(
            flops=10 * ROWS * D * R, bytes_accessed=24 << 20, transcendentals=2 * ROWS * R
        ),
    )(*arrays)


def solution(mesh):
    return jax.shard_map(
        per_device,
        mesh=mesh,
        in_specs=(
            P("section", "rep", None, None),
            P("section", "rep", None, None),
            P("section", "rep", None),
            P("rep", None),
            P("rep", None, None),
            P("section", None),
            P("section", None),
            P("section", "rep", None),
            P("section", "rep", None),
        ),
        out_specs=(P("section", "rep", None, None), P("section", "rep", None)),
        check_vma=False,
    )
```

```python
import jax
import jax.numpy as jnp
from jax import lax
from jax.experimental import pallas as pl
from jax.experimental.pallas import tpu as pltpu
from jax.sharding import PartitionSpec as P

EPSILON = 1e-05
HALF_ROOT = 0.7071067811865476
DENSITY = 0.3989422804014327
MESH = pl.DeviceIdType.MESH

D = 9216
R = 256
TOK = 64
ROWS = 128
NSEC = 8
NZ = 8
QUAD = D // NZ
SHARD = QUAD // 4
HALF = SHARD // 2
BLK = 16
NBLK = ROWS // BLK
ECH = 8
ECW = D // ECH
NSEM = 128
F32 = jnp.float32
BF16 = jnp.bfloat16


def nn(left, right):
    return lax.dot_general(left, right, (((1,), (0,)), ((), ())), preferred_element_type=F32)


def nt(left, right):
    return lax.dot_general(left, right, (((1,), (1,)), ((), ())), preferred_element_type=F32)


def tn(left, right):
    return lax.dot_general(left, right, (((0,), (0,)), ((), ())), preferred_element_type=F32)


def kernel(
    hist_h, codes_h, scales, ids, cot_h, gain, bias, wd_h, wu_h,
    ig_h, ag_h,
    hist, codes, xin, norm, wd, wu, grad, res,
    acc, slopes, qmat, ugain, hidden, acts, mean_s, inv_s, scol,
    gather_n, gather_g, gather_h, gather_a, total, tsend, trecv, xsend, xrecv, final,
    ss, rs, css, crs, gss, grs, ass, ars, osem, lsem,
):
    sec = lax.axis_index("section")
    rep = lax.axis_index("rep")
    z = rep // 4
    xl = (rep // 2) % 2
    core = rep % 2
    oxl = 1 - xl
    ocore = 1 - core

    def zi(step):
        return (z + step + NZ) % NZ

    def at_z(step):
        return (sec, zi(step) * 4 + xl * 2 + core)

    up, down = at_z(1), at_z(-1)
    side = (sec, z * 4 + oxl * 2 + core)
    twin = (sec, z * 4 + xl * 2 + ocore)
    below = (jnp.maximum(sec - 1, 0), rep)
    above = (jnp.minimum(sec + 1, NSEC - 1), rep)

    names = {}
    pending = []

    def sid(name):
        return names.setdefault(name, len(names))

    def link(name, src, dst, device):
        index = sid(name)
        return pltpu.make_async_remote_copy(
            src_ref=src, dst_ref=dst, send_sem=ss.at[index], recv_sem=rs.at[index],
            device_id=device, device_id_type=MESH,
        )

    def put(name, src, dst, device):
        copy = link(name, src, dst, device)
        copy.start()
        pending.append(copy)

    def got(name, dst, device):
        link(name, dst, dst, device).wait_recv()

    loads = [
        pltpu.make_async_copy(hist_h.at[0], hist, lsem.at[0]),
        pltpu.make_async_copy(codes_h.at[0], codes, lsem.at[1]),
        pltpu.make_async_copy(wd_h.at[0], wd.at[z, xl, core], lsem.at[2]),
        pltpu.make_async_copy(wu_h.at[0], wu.at[z, xl, core], lsem.at[3]),
    ]
    for load in loads:
        load.start()

    def seed(m):
        return pltpu.make_async_copy(cot_h.at[m], grad.at[pl.ds(m * TOK, TOK)], lsem.at[4 + m])

    @pl.when(sec == NSEC - 1)
    def _():
        for m in range(2):
            seed(m).start()

    barrier = pltpu.get_barrier_semaphore()
    ring = [at_z(step) for step in range(1, NZ)]
    for device in (*ring, side, twin):
        pl.semaphore_signal(barrier, inc=1, device_id=device, device_id_type=MESH)

    @pl.when(sec > 0)
    def _():
        pl.semaphore_signal(barrier, inc=1, device_id=below, device_id_type=MESH)

    @pl.when(sec < NSEC - 1)
    def _():
        pl.semaphore_signal(barrier, inc=1, device_id=above, device_id_type=MESH)

    @pl.when((sec > 0) & (sec < NSEC - 1))
    def _():
        pl.semaphore_wait(barrier, len(ring) + 4)

    @pl.when((sec == 0) | (sec == NSEC - 1))
    def _():
        pl.semaphore_wait(barrier, len(ring) + 3)

    own_d, own_u = wd.at[z, xl, core], wu.at[z, xl, core]
    put("Ux0", wu_h.at[0], own_u, side)
    put("Dz+0", wd_h.at[0], own_d, up)
    put("Dz-0", wd_h.at[0], own_d, down)
    put("Uz+0s", wu_h.at[0], own_u, up)
    put("Uz-0s", wu_h.at[0], own_u, down)
    put("Dx0", wd_h.at[0], own_d, side)
    put("Ds0", wd_h.at[0], own_d, twin)
    put("Us0", wu_h.at[0], own_u, twin)

    for load in loads[:2]:
        load.wait()

    eye = (
        lax.broadcasted_iota(jnp.int32, (TOK, TOK), 0)
        == lax.broadcasted_iota(jnp.int32, (TOK, TOK), 1)
    )
    for m in range(2):
        row = scales[0, pl.ds(m, 1), :]
        scol[pl.ds(m * TOK, TOK), :] = jnp.sum(
            jnp.where(eye, row, 0.0), axis=1, keepdims=True
        )

    def rebuild(i):
        rows = pl.ds(pl.multiple_of(i * BLK, BLK), BLK)
        m = i // (TOK // BLK)
        inner = pl.ds(pl.multiple_of((i % (TOK // BLK)) * BLK, BLK), BLK)
        step = scol[rows, :]
        pick = ids[0, m]
        total = jnp.zeros((BLK, 1), F32)
        for e in range(ECH):
            cols = pl.ds(e * ECW, ECW)
            value = hist[pick, inner, cols].astype(F32) + step * codes[m, inner, cols].astype(F32)
            value = value.astype(BF16)
            xin[rows, cols] = value
            total = total + jnp.sum(value.astype(F32), axis=1, keepdims=True)
        mean = total * (1.0 / D)
        square = jnp.zeros((BLK, 1), F32)
        for e in range(ECH):
            cols = pl.ds(e * ECW, ECW)
            centred = xin[rows, cols].astype(F32) - mean
            square = square + jnp.sum(centred * centred, axis=1, keepdims=True)
        inv = lax.rsqrt(square * (1.0 / D) + EPSILON)
        mean_s[rows, :] = mean
        inv_s[rows, :] = inv
        for e in range(ECH):
            cols = pl.ds(e * ECW, ECW)
            scaled = (xin[rows, cols].astype(F32) - mean) * inv
            norm[rows, cols] = (scaled * gain[:, cols] + bias[:, cols]).astype(BF16)

    def rebuild_some(first, count):
        def step(i, carry):
            rebuild(first + i)
            return carry

        lax.fori_loop(0, count, step, 0)

    def extra_rows():
        line = lax.broadcasted_iota(jnp.int32, (BLK, ECW), 0)
        for e in range(ECH):
            cols = pl.ds(e * ECW, ECW)
            g, b = gain[:, cols], bias[:, cols]
            g_hi, b_hi = g.astype(BF16).astype(F32), b.astype(BF16).astype(F32)
            stack = jnp.where(line == 0, g_hi, 0.0)
            stack = jnp.where(line == 1, g - g_hi, stack)
            stack = jnp.where(line == 2, b_hi, stack)
            stack = jnp.where(line == 3, b - b_hi, stack)
            norm[pl.ds(ROWS, BLK), cols] = stack.astype(BF16)

    def quad_cols(q):
        return pl.ds(pl.multiple_of(q * QUAD, QUAD), QUAD)

    def forward(q, first=False):
        part = nn(norm[:, quad_cols(q)], wd[q].reshape(QUAD, R))
        if first:
            acc[...] = part
        else:
            acc[...] += part

    extra_rows()
    got("Ux0", wu.at[z, oxl, core], side)
    put("Uz+0p", wu.at[z, oxl, core], wu.at[z, oxl, core], up)
    put("Uz-0p", wu.at[z, oxl, core], wu.at[z, oxl, core], down)
    put("Uxs0", wu.at[z, oxl, core], wu.at[z, oxl, core], twin)
    got("Dx0", wd.at[z, oxl, core], side)
    put("Dxs0", wd.at[z, oxl, core], wd.at[z, oxl, core], twin)
    rebuild_some(0, 2)

    def piece(ref, direction, dist, e, c):
        q = zi(-dist if direction == "+" else dist)
        if dist < 4 or ref is wu:
            return ref.at[q, e, c]
        first = 0 if direction == "+" else HALF
        return ref.at[q, e, c, pl.ds(first, HALF)]

    def onward(ref, direction, dist, e, c):
        q = zi(-dist if direction == "+" else dist)
        if dist < 3 or ref is wu:
            return ref.at[q, e, c]
        first = 0 if direction == "+" else HALF
        return ref.at[q, e, c, pl.ds(first, HALF)]

    ways = (("+", up, down), ("-", down, up))

    def down_ready(dist):
        if dist == 0:
            got("Ds0", wd.at[z, xl, ocore], twin)
            got("Dxs0", wd.at[z, oxl, ocore], twin)
            return
        for way, _, _ in ways:
            got(f"Ds{way}{dist}", piece(wd, way, dist, xl, ocore), twin)
            got(f"Dxs{way}{dist}", piece(wd, way, dist, oxl, ocore), twin)

    for dist in range(1, 5):
        for way, ahead, behind in ways:
            part = piece(wd, way, dist, xl, core)
            got(f"Dz{way}{dist - 1}", part, behind)
            if dist < 4:
                more = onward(wd, way, dist, xl, core)
                put(f"Dz{way}{dist}", more, more, ahead)
            put(f"Dx{way}{dist}", part, part, side)
            put(f"Ds{way}{dist}", part, part, twin)
        for which, e in (("s", xl), ("p", oxl)):
            for way, ahead, behind in ways:
                if dist == 4 and (way == "+") != (which == "s"):
                    continue
                part = piece(wu, way, dist, e, core)
                got(f"Uz{way}{dist - 1}{which}", part, behind)
                if dist < 3 or (dist == 3 and (way == "+") == (which == "s")):
                    put(f"Uz{way}{dist}{which}", part, part, ahead)
                put(f"Us{way}{dist}{which}", part, part, twin)
        for way, ahead, behind in ways:
            part = piece(wd, way, dist, oxl, core)
            got(f"Dx{way}{dist}", part, side)
            put(f"Dxs{way}{dist}", part, part, twin)
        if dist < 4:
            rebuild_some(2 * dist, 2)
        if dist == 3:
            loads[2].wait()
            down_ready(0)
            forward(zi(0), True)
            down_ready(1)
            forward(zi(-1))
            forward(zi(1))
    for dist in (2, 3):
        down_ready(dist)
        forward(zi(-dist))
        forward(zi(dist))
    down_ready(4)
    forward(zi(4))

    shift = acc[ROWS + 2 : ROWS + 3, :] + acc[ROWS + 3 : ROWS + 4, :]
    ugain[...] = acc[ROWS : ROWS + 1, :] + acc[ROWS + 1 : ROWS + 2, :]
    for i in range(4):
        rows = pl.ds(i * 32, 32)
        preact = acc[rows, :]
        cdf = 0.5 * (1.0 + lax.erf(preact * HALF_ROOT))
        bump = DENSITY * jnp.exp(-0.5 * preact * preact)
        hidden[rows, :] = (preact * cdf).astype(BF16)
        slopes[rows, :] = cdf + preact * bump
        qmat[rows, :] = preact - shift

    loads[3].wait()
    got("Us0", wu.at[z, xl, ocore], twin)
    got("Uxs0", wu.at[z, oxl, ocore], twin)
    for dist in range(1, 5):
        for which, e in (("s", xl), ("p", oxl)):
            for way, _, _ in ways:
                if dist == 4 and (way == "+") != (which == "s"):
                    continue
                got(f"Us{way}{dist}{which}", piece(wu, way, dist, e, ocore), twin)

    @pl.when(sec == NSEC - 1)
    def _():
        for m in range(2):
            seed(m).wait()

    own_n = pltpu.make_async_copy(
        norm.at[pl.ds(0, ROWS), quad_cols(z)], gather_n.at[z], lsem.at[7]
    )
    own_n.start()

    def spread_norm(step):
        return link(
            f"N{step}", norm.at[pl.ds(0, ROWS), quad_cols(zi(step))], gather_n.at[z], at_z(step)
        )

    def tour_rows(first, count, dist, way):
        if dist < 4:
            return pl.ds(first, count)
        half = count // (2 * BLK) * BLK
        return pl.ds(first, half) if way == "+" else pl.ds(first + half, count - half)

    def tour_links(name, src, dst, first, count, stage):
        copies = []
        for way, ahead, _ in ways:
            q = zi(-stage if way == "+" else stage)
            rows = tour_rows(first, count, stage + 1, way)
            held = src.at[rows] if stage == 0 else dst.at[q, rows]
            copies.append(link(f"{name}{way}{stage}", held, dst.at[q, rows], ahead))
        return copies

    def tour(name, src, dst, first, count, stage):
        if stage > 0:
            for way, _, behind in ways:
                q = zi(-stage if way == "+" else stage)
                rows = tour_rows(first, count, stage, way)
                got(f"{name}{way}{stage - 1}", dst.at[q, rows], behind)
        if stage < 4:
            for copy in tour_links(name, src, dst, first, count, stage):
                copy.start()

    def tour_sent(name, src, dst, first, count):
        for stage in range(4):
            for copy in tour_links(name, src, dst, first, count, stage):
                copy.wait_send()

    gather_h[z] = hidden[...]

    @pl.when(sec <= 1)
    def _():
        for stage in range(5):
            tour("Ha", hidden, gather_h, 0, ROWS, stage)
            for step in ((4,), (3, 5), (2, 6), (1, 7), ())[stage]:
                spread_norm(step).start()

    @pl.when(sec > 1)
    def _():
        for step in range(1, NZ):
            spread_norm(step).start()

    def rows_of(i):
        return pl.ds(pl.multiple_of(i * BLK, BLK), BLK)

    def hop(i, n, src):
        part = (rows_of(i), quad_cols(zi(n + 1)))
        index = i * NZ + n
        return pltpu.make_async_remote_copy(
            src_ref=src.at[part], dst_ref=grad.at[part],
            send_sem=css.at[index], recv_sem=crs.at[index],
            device_id=below, device_id_type=MESH,
        )

    def spread_grad(i, n, landing):
        index = i * NZ + n
        return pltpu.make_async_remote_copy(
            src_ref=grad.at[rows_of(i), quad_cols(zi(n + 1))],
            dst_ref=gather_g.at[landing, rows_of(i)],
            send_sem=gss.at[index], recv_sem=grs.at[index],
            device_id=at_z(n + 1), device_id_type=MESH,
        )

    def own_grad(i):
        return pltpu.make_async_copy(
            grad.at[rows_of(i), quad_cols(z)], gather_g.at[z, rows_of(i)],
            grs.at[i * NZ + NZ - 1],
        )

    def spread_act(i, n, landing):
        index = i * NZ + n
        return pltpu.make_async_remote_copy(
            src_ref=acts.at[rows_of(i)], dst_ref=gather_a.at[landing, rows_of(i)],
            send_sem=ass.at[index], recv_sem=ars.at[index],
            device_id=at_z(n + 1), device_id_type=MESH,
        )

    def keep(i):
        inner = pl.ds(pl.multiple_of((i % (TOK // BLK)) * BLK, BLK), BLK)
        return pltpu.make_async_copy(
            res.at[rows_of(i)], ig_h.at[0, i // (TOK // BLK), inner], osem.at[i]
        )

    def chain(i, carry):
        rows = rows_of(i)
        lift = jnp.zeros((BLK, R), F32)
        for n in range(NZ):
            q = zi(n + 1)

            @pl.when(sec < NSEC - 1)
            def _():
                hop(i, n, grad).wait_recv()

            if n < NZ - 1:
                spread_grad(i, n, z).start()
            else:
                own_grad(i).start()
            lift = lift + nn(grad[rows, quad_cols(q)], wu[q].reshape(QUAD, R))
        act = (lift * slopes[rows, :]).astype(BF16)
        acts[rows, :] = act
        gather_a[z, rows, :] = act

        @pl.when(sec <= 1)
        def _():
            for n in range(NZ - 1):
                spread_act(i, n, z).start()

        wide = act.astype(F32)
        m1 = jnp.sum(wide * ugain[...], axis=1, keepdims=True) * (1.0 / D)
        m2 = jnp.sum(wide * qmat[rows, :], axis=1, keepdims=True) * (1.0 / D)
        mean, inv = mean_s[rows, :], inv_s[rows, :]
        tilt = inv * inv * m2
        base = inv * m1 - mean * tilt
        for n in range(NZ):
            q = zi(n + 1)
            cols = quad_cols(q)
            back = nt(act, wd[q].reshape(QUAD, R))
            value = (
                grad[rows, cols].astype(F32) + inv * (back * gain[:, cols]) - base
                - xin[rows, cols].astype(F32) * tilt
            )
            res[rows, cols] = value.astype(BF16)

            @pl.when(sec > 0)
            def _():
                hop(i, n, res).start()

        keep(i).start()
        return carry

    lax.fori_loop(0, NBLK, chain, 0)

    @pl.when(sec > 1)
    def _():
        for stage in range(5):
            tour("Ad", acts, gather_a, 0, ROWS, stage)
            tour("Hb", hidden, gather_h, 0, ROWS, stage)

    own_n.wait()
    for step in range(1, NZ):
        got(f"N{step}", gather_n.at[zi(-step)], at_z(-step))

    def arrived(h, i):
        for n in range(NZ - 1):
            if h == 1:
                spread_grad(i, n, zi(-(n + 1))).wait_recv()
            else:
                spread_act(i, n, zi(-(n + 1))).wait_recv()
        if h == 1:
            own_grad(i).wait()

    def add_terms(h, first, count):
        if h == 1:
            for i in range(first, first + count):
                arrived(1, i)
        else:
            @pl.when(sec <= 1)
            def _():
                for i in range(first, first + count):
                    arrived(0, i)

        rows = pl.ds(first * BLK, count * BLK)
        depth = NZ * count * BLK
        wide_ref, thin_ref = ((gather_n, gather_a), (gather_g, gather_h))[h]
        term = tn(
            wide_ref[:, rows, :].reshape(depth, QUAD), thin_ref[:, rows, :].reshape(depth, R)
        ).reshape(2, 2, SHARD, R)
        if first == 0:
            total[h] = term
        else:
            total[h] += term

    def to_twin(h):
        for e, which in ((oxl, "p"), (xl, "s")):
            tsend[h, e] = (total[h, e, ocore] * scale).astype(BF16)
            put(f"T{h}{which}", tsend.at[h, e], trecv.at[h, e], twin)

    scale = 1.0 / TOK
    for first, count in ((0, 3), (3, 3), (6, 1)):
        for h in (1, 0):
            add_terms(h, first, count)
    add_terms(1, 7, 1)
    to_twin(1)

    def to_side(h):
        got(f"T{h}p", trecv.at[h, oxl], twin)
        xsend[h] = (total[h, oxl, core] * scale + trecv[h, oxl].astype(F32)).astype(BF16)
        put(f"X{h}", xsend.at[h], xrecv.at[h], side)

    to_side(1)
    add_terms(0, 7, 1)
    to_twin(0)
    to_side(0)
    for h in (1, 0):
        got(f"T{h}s", trecv.at[h, xl], twin)
        total[h, xl, core] = total[h, xl, core] * scale + trecv[h, xl].astype(F32)
    for h in (1, 0):
        got(f"X{h}", xrecv.at[h], side)
        final[:, pl.ds(h * R, R)] = total[h, xl, core] + xrecv[h].astype(F32)
    store = pltpu.make_async_copy(final, ag_h.at[0], lsem.at[6])
    store.start()

    for step in range(1, NZ):
        spread_norm(step).wait_send()
    for copy in pending:
        copy.wait_send()

    @pl.when(sec <= 1)
    def _():
        tour_sent("Ha", hidden, gather_h, 0, ROWS)

    @pl.when(sec > 1)
    def _():
        tour_sent("Ad", acts, gather_a, 0, ROWS)
        tour_sent("Hb", hidden, gather_h, 0, ROWS)

    def settle(i, carry):
        @pl.when(sec > 0)
        def _():
            for n in range(NZ):
                hop(i, n, res).wait_send()

        for n in range(NZ - 1):
            spread_grad(i, n, z).wait_send()

        @pl.when(sec <= 1)
        def _():
            for n in range(NZ - 1):
                spread_act(i, n, z).wait_send()

        keep(i).wait()
        return carry

    lax.fori_loop(0, NBLK, settle, 0)
    store.wait()
    assert len(names) <= NSEM


def per_device(*arrays):
    vmem = pl.BlockSpec(memory_space=pltpu.VMEM)
    smem = pl.BlockSpec(memory_space=pltpu.SMEM)
    hbm = pl.BlockSpec(memory_space=pl.ANY)
    return pl.pallas_call(
        kernel,
        out_shape=(
            jax.ShapeDtypeStruct((1, 2, TOK, D), BF16),
            jax.ShapeDtypeStruct((1, SHARD, 2 * R), F32),
        ),
        in_specs=[hbm, hbm, vmem, smem, hbm, vmem, vmem, hbm, hbm],
        out_specs=(hbm, hbm),
        scratch_shapes=[
            pltpu.VMEM((2, TOK, D), BF16),
            pltpu.VMEM((2, TOK, D), jnp.int32),
            pltpu.VMEM((ROWS, D), BF16),
            pltpu.VMEM((ROWS + BLK, D), BF16),
            pltpu.VMEM((NZ, 2, 2, SHARD, R), BF16),
            pltpu.VMEM((NZ, 2, 2, SHARD, R), BF16),
            pltpu.VMEM((ROWS, D), BF16),
            pltpu.VMEM((ROWS, D), BF16),
            pltpu.VMEM((ROWS + BLK, R), F32),
            pltpu.VMEM((ROWS, R), F32),
            pltpu.VMEM((ROWS, R), F32),
            pltpu.VMEM((1, R), F32),
            pltpu.VMEM((ROWS, R), BF16),
            pltpu.VMEM((ROWS, R), BF16),
            pltpu.VMEM((ROWS, 1), F32),
            pltpu.VMEM((ROWS, 1), F32),
            pltpu.VMEM((ROWS, 1), F32),
            pltpu.VMEM((NZ, ROWS, QUAD), BF16),
            pltpu.VMEM((NZ, ROWS, QUAD), BF16),
            pltpu.VMEM((NZ, ROWS, R), BF16),
            pltpu.VMEM((NZ, ROWS, R), BF16),
            pltpu.VMEM((2, 2, 2, SHARD, R), F32),
            pltpu.VMEM((2, 2, SHARD, R), BF16),
            pltpu.VMEM((2, 2, SHARD, R), BF16),
            pltpu.VMEM((2, SHARD, R), BF16),
            pltpu.VMEM((2, SHARD, R), BF16),
            pltpu.VMEM((SHARD, 2 * R), F32),
            pltpu.SemaphoreType.DMA((NSEM,)),
            pltpu.SemaphoreType.DMA((NSEM,)),
            pltpu.SemaphoreType.DMA((NBLK * NZ,)),
            pltpu.SemaphoreType.DMA((NBLK * NZ,)),
            pltpu.SemaphoreType.DMA((NBLK * NZ,)),
            pltpu.SemaphoreType.DMA((NBLK * NZ,)),
            pltpu.SemaphoreType.DMA((NBLK * NZ,)),
            pltpu.SemaphoreType.DMA((NBLK * NZ,)),
            pltpu.SemaphoreType.DMA((NBLK,)),
            pltpu.SemaphoreType.DMA((8,)),
        ],
        compiler_params=pltpu.CompilerParams(
            collective_id=0, has_side_effects=True, vmem_limit_bytes=60 << 20
        ),
        cost_estimate=pl.CostEstimate(
            flops=10 * ROWS * D * R, bytes_accessed=24 << 20, transcendentals=2 * ROWS * R
        ),
    )(*arrays)


def solution(mesh):
    return jax.shard_map(
        per_device,
        mesh=mesh,
        in_specs=(
            P("section", "rep", None, None),
            P("section", "rep", None, None),
            P("section", "rep", None),
            P("rep", None),
            P("rep", None, None),
            P("section", None),
            P("section", None),
            P("section", "rep", None),
            P("section", "rep", None),
        ),
        out_specs=(P("section", "rep", None, None), P("section", "rep", None)),
        check_vma=False,
    )
```

```python
import jax
import jax.numpy as jnp
from jax import lax
from jax.experimental import pallas as pl
from jax.experimental.pallas import tpu as pltpu
from jax.sharding import PartitionSpec as P

EPSILON = 1e-05
HALF_ROOT = 0.7071067811865476
DENSITY = 0.3989422804014327
MESH = pl.DeviceIdType.MESH

D = 9216
R = 256
TOK = 64
ROWS = 128
NSEC = 8
NZ = 8
QUAD = D // NZ
SHARD = QUAD // 4
HALF = SHARD // 2
BLK = 16
NBLK = ROWS // BLK
STEPS = (4, 3, 5, 2, 6, 1, 7, 0)
ECH = 8
ECW = D // ECH
NSEM = 128
F32 = jnp.float32
BF16 = jnp.bfloat16


def nn(left, right):
    return lax.dot_general(left, right, (((1,), (0,)), ((), ())), preferred_element_type=F32)


def nt(left, right):
    return lax.dot_general(left, right, (((1,), (1,)), ((), ())), preferred_element_type=F32)


def tn(left, right):
    return lax.dot_general(left, right, (((0,), (0,)), ((), ())), preferred_element_type=F32)


def kernel(
    hist_h, codes_h, scales, ids, cot_h, gain, bias, wd_h, wu_h,
    ig_h, ag_h,
    hist, codes, xin, norm, wd, wu, grad, res,
    acc, slopes, qmat, ugain, hidden, acts, mean_s, inv_s, scol,
    gather_n, gather_g, gather_h, gather_a, total, tsend, trecv, xsend, xrecv, final,
    ss, rs, css, crs, gss, grs, ass, ars, osem, lsem,
):
    sec = lax.axis_index("section")
    rep = lax.axis_index("rep")
    z = rep // 4
    xl = (rep // 2) % 2
    core = rep % 2
    oxl = 1 - xl
    ocore = 1 - core

    def zi(step):
        return (z + step + NZ) % NZ

    def at_z(step):
        return (sec, zi(step) * 4 + xl * 2 + core)

    up, down = at_z(1), at_z(-1)
    side = (sec, z * 4 + oxl * 2 + core)
    twin = (sec, z * 4 + xl * 2 + ocore)
    below = (jnp.maximum(sec - 1, 0), rep)
    above = (jnp.minimum(sec + 1, NSEC - 1), rep)

    names = {}
    pending = []

    def sid(name):
        return names.setdefault(name, len(names))

    def link(name, src, dst, device):
        index = sid(name)
        return pltpu.make_async_remote_copy(
            src_ref=src, dst_ref=dst, send_sem=ss.at[index], recv_sem=rs.at[index],
            device_id=device, device_id_type=MESH,
        )

    def put(name, src, dst, device):
        copy = link(name, src, dst, device)
        copy.start()
        pending.append(copy)

    def got(name, dst, device):
        link(name, dst, dst, device).wait_recv()

    loads = [
        pltpu.make_async_copy(hist_h.at[0], hist, lsem.at[0]),
        pltpu.make_async_copy(codes_h.at[0], codes, lsem.at[1]),
        pltpu.make_async_copy(wd_h.at[0], wd.at[z, xl, core], lsem.at[2]),
        pltpu.make_async_copy(wu_h.at[0], wu.at[z, xl, core], lsem.at[3]),
    ]
    for load in loads:
        load.start()

    def seed(m):
        return pltpu.make_async_copy(cot_h.at[m], grad.at[pl.ds(m * TOK, TOK)], lsem.at[4 + m])

    @pl.when(sec == NSEC - 1)
    def _():
        for m in range(2):
            seed(m).start()

    barrier = pltpu.get_barrier_semaphore()
    ring = [at_z(step) for step in range(1, NZ)]
    for device in (*ring, side, twin):
        pl.semaphore_signal(barrier, inc=1, device_id=device, device_id_type=MESH)

    @pl.when(sec > 0)
    def _():
        pl.semaphore_signal(barrier, inc=1, device_id=below, device_id_type=MESH)

    @pl.when(sec < NSEC - 1)
    def _():
        pl.semaphore_signal(barrier, inc=1, device_id=above, device_id_type=MESH)

    @pl.when((sec > 0) & (sec < NSEC - 1))
    def _():
        pl.semaphore_wait(barrier, len(ring) + 4)

    @pl.when((sec == 0) | (sec == NSEC - 1))
    def _():
        pl.semaphore_wait(barrier, len(ring) + 3)

    own_d, own_u = wd.at[z, xl, core], wu.at[z, xl, core]
    put("Ux0", wu_h.at[0], own_u, side)
    put("Dz+0", wd_h.at[0], own_d, up)
    put("Dz-0", wd_h.at[0], own_d, down)
    put("Uz+0s", wu_h.at[0], own_u, up)
    put("Uz-0s", wu_h.at[0], own_u, down)
    put("Dx0", wd_h.at[0], own_d, side)
    put("Ds0", wd_h.at[0], own_d, twin)
    put("Us0", wu_h.at[0], own_u, twin)

    for load in loads[:2]:
        load.wait()

    eye = (
        lax.broadcasted_iota(jnp.int32, (TOK, TOK), 0)
        == lax.broadcasted_iota(jnp.int32, (TOK, TOK), 1)
    )
    for m in range(2):
        row = scales[0, pl.ds(m, 1), :]
        scol[pl.ds(m * TOK, TOK), :] = jnp.sum(
            jnp.where(eye, row, 0.0), axis=1, keepdims=True
        )

    def rebuild(i):
        rows = pl.ds(pl.multiple_of(i * BLK, BLK), BLK)
        m = i // (TOK // BLK)
        inner = pl.ds(pl.multiple_of((i % (TOK // BLK)) * BLK, BLK), BLK)
        step = scol[rows, :]
        pick = ids[0, m]
        total = jnp.zeros((BLK, 1), F32)
        for e in range(ECH):
            cols = pl.ds(e * ECW, ECW)
            value = hist[pick, inner, cols].astype(F32) + step * codes[m, inner, cols].astype(F32)
            value = value.astype(BF16)
            xin[rows, cols] = value
            total = total + jnp.sum(value.astype(F32), axis=1, keepdims=True)
        mean = total * (1.0 / D)
        square = jnp.zeros((BLK, 1), F32)
        for e in range(ECH):
            cols = pl.ds(e * ECW, ECW)
            centred = xin[rows, cols].astype(F32) - mean
            square = square + jnp.sum(centred * centred, axis=1, keepdims=True)
        inv = lax.rsqrt(square * (1.0 / D) + EPSILON)
        mean_s[rows, :] = mean
        inv_s[rows, :] = inv
        for e in range(ECH):
            cols = pl.ds(e * ECW, ECW)
            scaled = (xin[rows, cols].astype(F32) - mean) * inv
            norm[rows, cols] = (scaled * gain[:, cols] + bias[:, cols]).astype(BF16)

    def rebuild_some(first, count):
        def step(i, carry):
            rebuild(first + i)
            return carry

        lax.fori_loop(0, count, step, 0)

    def extra_rows():
        line = lax.broadcasted_iota(jnp.int32, (BLK, ECW), 0)
        for e in range(ECH):
            cols = pl.ds(e * ECW, ECW)
            g, b = gain[:, cols], bias[:, cols]
            g_hi, b_hi = g.astype(BF16).astype(F32), b.astype(BF16).astype(F32)
            stack = jnp.where(line == 0, g_hi, 0.0)
            stack = jnp.where(line == 1, g - g_hi, stack)
            stack = jnp.where(line == 2, b_hi, stack)
            stack = jnp.where(line == 3, b - b_hi, stack)
            norm[pl.ds(ROWS, BLK), cols] = stack.astype(BF16)

    def quad_cols(q):
        return pl.ds(pl.multiple_of(q * QUAD, QUAD), QUAD)

    def forward(q, first=False):
        part = nn(norm[:, quad_cols(q)], wd[q].reshape(QUAD, R))
        if first:
            acc[...] = part
        else:
            acc[...] += part

    extra_rows()
    got("Ux0", wu.at[z, oxl, core], side)
    put("Uz+0p", wu.at[z, oxl, core], wu.at[z, oxl, core], up)
    put("Uz-0p", wu.at[z, oxl, core], wu.at[z, oxl, core], down)
    put("Uxs0", wu.at[z, oxl, core], wu.at[z, oxl, core], twin)
    got("Dx0", wd.at[z, oxl, core], side)
    put("Dxs0", wd.at[z, oxl, core], wd.at[z, oxl, core], twin)
    rebuild_some(0, 2)

    def piece(ref, direction, dist, e, c):
        q = zi(-dist if direction == "+" else dist)
        if dist < 4 or ref is wu:
            return ref.at[q, e, c]
        first = 0 if direction == "+" else HALF
        return ref.at[q, e, c, pl.ds(first, HALF)]

    def onward(ref, direction, dist, e, c):
        q = zi(-dist if direction == "+" else dist)
        if dist < 3 or ref is wu:
            return ref.at[q, e, c]
        first = 0 if direction == "+" else HALF
        return ref.at[q, e, c, pl.ds(first, HALF)]

    ways = (("+", up, down), ("-", down, up))

    def down_ready(dist):
        if dist == 0:
            got("Ds0", wd.at[z, xl, ocore], twin)
            got("Dxs0", wd.at[z, oxl, ocore], twin)
            return
        for way, _, _ in ways:
            got(f"Ds{way}{dist}", piece(wd, way, dist, xl, ocore), twin)
            got(f"Dxs{way}{dist}", piece(wd, way, dist, oxl, ocore), twin)

    for dist in range(1, 5):
        for way, ahead, behind in ways:
            part = piece(wd, way, dist, xl, core)
            got(f"Dz{way}{dist - 1}", part, behind)
            if dist < 4:
                more = onward(wd, way, dist, xl, core)
                put(f"Dz{way}{dist}", more, more, ahead)
            put(f"Dx{way}{dist}", part, part, side)
            put(f"Ds{way}{dist}", part, part, twin)
        for which, e in (("s", xl), ("p", oxl)):
            for way, ahead, behind in ways:
                if dist == 4 and (way == "+") != (which == "s"):
                    continue
                part = piece(wu, way, dist, e, core)
                got(f"Uz{way}{dist - 1}{which}", part, behind)
                if dist < 3 or (dist == 3 and (way == "+") == (which == "s")):
                    put(f"Uz{way}{dist}{which}", part, part, ahead)
                put(f"Us{way}{dist}{which}", part, part, twin)
        for way, ahead, behind in ways:
            part = piece(wd, way, dist, oxl, core)
            got(f"Dx{way}{dist}", part, side)
            put(f"Dxs{way}{dist}", part, part, twin)
        if dist < 4:
            rebuild_some(2 * dist, 2)
        if dist == 3:
            loads[2].wait()
            down_ready(0)
            forward(zi(0), True)
            down_ready(1)
            forward(zi(-1))
            forward(zi(1))
    for dist in (2, 3):
        down_ready(dist)
        forward(zi(-dist))
        forward(zi(dist))
    down_ready(4)
    forward(zi(4))

    shift = acc[ROWS + 2 : ROWS + 3, :] + acc[ROWS + 3 : ROWS + 4, :]
    ugain[...] = acc[ROWS : ROWS + 1, :] + acc[ROWS + 1 : ROWS + 2, :]
    for i in range(4):
        rows = pl.ds(i * 32, 32)
        preact = acc[rows, :]
        cdf = 0.5 * (1.0 + lax.erf(preact * HALF_ROOT))
        bump = DENSITY * jnp.exp(-0.5 * preact * preact)
        hidden[rows, :] = (preact * cdf).astype(BF16)
        slopes[rows, :] = cdf + preact * bump
        qmat[rows, :] = preact - shift

    loads[3].wait()
    got("Us0", wu.at[z, xl, ocore], twin)
    got("Uxs0", wu.at[z, oxl, ocore], twin)
    for dist in range(1, 5):
        for which, e in (("s", xl), ("p", oxl)):
            for way, _, _ in ways:
                if dist == 4 and (way == "+") != (which == "s"):
                    continue
                got(f"Us{way}{dist}{which}", piece(wu, way, dist, e, ocore), twin)

    @pl.when(sec == NSEC - 1)
    def _():
        for m in range(2):
            seed(m).wait()

    own_n = pltpu.make_async_copy(
        norm.at[pl.ds(0, ROWS), quad_cols(z)], gather_n.at[z], lsem.at[7]
    )
    own_n.start()

    def spread_norm(step):
        return link(
            f"N{step}", norm.at[pl.ds(0, ROWS), quad_cols(zi(step))], gather_n.at[z], at_z(step)
        )

    def tour_rows(first, count, dist, way):
        if dist < 4:
            return pl.ds(first, count)
        half = count // (2 * BLK) * BLK
        return pl.ds(first, half) if way == "+" else pl.ds(first + half, count - half)

    def tour_links(name, src, dst, first, count, stage):
        copies = []
        for way, ahead, _ in ways:
            q = zi(-stage if way == "+" else stage)
            rows = tour_rows(first, count, stage + 1, way)
            held = src.at[rows] if stage == 0 else dst.at[q, rows]
            copies.append(link(f"{name}{way}{stage}", held, dst.at[q, rows], ahead))
        return copies

    def tour(name, src, dst, first, count, stage):
        if stage > 0:
            for way, _, behind in ways:
                q = zi(-stage if way == "+" else stage)
                rows = tour_rows(first, count, stage, way)
                got(f"{name}{way}{stage - 1}", dst.at[q, rows], behind)
        if stage < 4:
            for copy in tour_links(name, src, dst, first, count, stage):
                copy.start()

    def tour_sent(name, src, dst, first, count):
        for stage in range(4):
            for copy in tour_links(name, src, dst, first, count, stage):
                copy.wait_send()

    gather_h[z] = hidden[...]

    @pl.when(sec <= 1)
    def _():
        for stage in range(5):
            tour("Ha", hidden, gather_h, 0, ROWS, stage)
            for step in ((4,), (3, 5), (2, 6), (1, 7), ())[stage]:
                spread_norm(step).start()

    @pl.when(sec > 1)
    def _():
        for step in range(1, NZ):
            spread_norm(step).start()

    def rows_of(i):
        return pl.ds(pl.multiple_of(i * BLK, BLK), BLK)

    def hop(i, n, src):
        part = (rows_of(i), quad_cols(zi(STEPS[n])))
        index = i * NZ + n
        return pltpu.make_async_remote_copy(
            src_ref=src.at[part], dst_ref=grad.at[part],
            send_sem=css.at[index], recv_sem=crs.at[index],
            device_id=below, device_id_type=MESH,
        )

    def spread_grad(i, n, landing):
        index = i * NZ + n
        return pltpu.make_async_remote_copy(
            src_ref=grad.at[rows_of(i), quad_cols(zi(STEPS[n]))],
            dst_ref=gather_g.at[landing, rows_of(i)],
            send_sem=gss.at[index], recv_sem=grs.at[index],
            device_id=at_z(STEPS[n]), device_id_type=MESH,
        )

    def own_grad(i):
        return pltpu.make_async_copy(
            grad.at[rows_of(i), quad_cols(z)], gather_g.at[z, rows_of(i)],
            grs.at[i * NZ + NZ - 1],
        )

    def spread_act(i, n, landing):
        index = i * NZ + n
        return pltpu.make_async_remote_copy(
            src_ref=acts.at[rows_of(i)], dst_ref=gather_a.at[landing, rows_of(i)],
            send_sem=ass.at[index], recv_sem=ars.at[index],
            device_id=at_z(STEPS[n]), device_id_type=MESH,
        )

    def keep(i):
        inner = pl.ds(pl.multiple_of((i % (TOK // BLK)) * BLK, BLK), BLK)
        return pltpu.make_async_copy(
            res.at[rows_of(i)], ig_h.at[0, i // (TOK // BLK), inner], osem.at[i]
        )

    def chain(i, carry):
        rows = rows_of(i)
        lift = jnp.zeros((BLK, R), F32)
        for n in range(NZ):
            q = zi(STEPS[n])

            @pl.when(sec < NSEC - 1)
            def _():
                hop(i, n, grad).wait_recv()

            if n < NZ - 1:
                spread_grad(i, n, z).start()
            else:
                own_grad(i).start()
            lift = lift + nn(grad[rows, quad_cols(q)], wu[q].reshape(QUAD, R))
        act = (lift * slopes[rows, :]).astype(BF16)
        acts[rows, :] = act
        gather_a[z, rows, :] = act

        @pl.when(sec <= 1)
        def _():
            for n in range(NZ - 1):
                spread_act(i, n, z).start()

        wide = act.astype(F32)
        m1 = jnp.sum(wide * ugain[...], axis=1, keepdims=True) * (1.0 / D)
        m2 = jnp.sum(wide * qmat[rows, :], axis=1, keepdims=True) * (1.0 / D)
        mean, inv = mean_s[rows, :], inv_s[rows, :]
        tilt = inv * inv * m2
        base = inv * m1 - mean * tilt
        for n in range(NZ):
            q = zi(STEPS[n])
            cols = quad_cols(q)
            back = nt(act, wd[q].reshape(QUAD, R))
            value = (
                grad[rows, cols].astype(F32) + inv * (back * gain[:, cols]) - base
                - xin[rows, cols].astype(F32) * tilt
            )
            res[rows, cols] = value.astype(BF16)

            @pl.when(sec > 0)
            def _():
                hop(i, n, res).start()

        keep(i).start()
        return carry

    lax.fori_loop(0, NBLK, chain, 0)

    @pl.when(sec > 1)
    def _():
        for stage in range(5):
            tour("Ad", acts, gather_a, 0, ROWS, stage)
            tour("Hb", hidden, gather_h, 0, ROWS, stage)

    own_n.wait()
    for step in range(1, NZ):
        got(f"N{step}", gather_n.at[zi(-step)], at_z(-step))

    def arrived(h, i):
        for n in range(NZ - 1):
            if h == 1:
                spread_grad(i, n, zi(-STEPS[n])).wait_recv()
            else:
                spread_act(i, n, zi(-STEPS[n])).wait_recv()
        if h == 1:
            own_grad(i).wait()

    def add_terms(h, first, count):
        if h == 1:
            for i in range(first, first + count):
                arrived(1, i)
        else:
            @pl.when(sec <= 1)
            def _():
                for i in range(first, first + count):
                    arrived(0, i)

        rows = pl.ds(first * BLK, count * BLK)
        depth = NZ * count * BLK
        wide_ref, thin_ref = ((gather_n, gather_a), (gather_g, gather_h))[h]
        term = tn(
            wide_ref[:, rows, :].reshape(depth, QUAD), thin_ref[:, rows, :].reshape(depth, R)
        ).reshape(2, 2, SHARD, R)
        if first == 0:
            total[h] = term
        else:
            total[h] += term

    def to_twin(h):
        for e, which in ((oxl, "p"), (xl, "s")):
            tsend[h, e] = (total[h, e, ocore] * scale).astype(BF16)
            put(f"T{h}{which}", tsend.at[h, e], trecv.at[h, e], twin)

    scale = 1.0 / TOK
    for first, count in ((0, 3), (3, 3), (6, 1)):
        for h in (1, 0):
            add_terms(h, first, count)
    add_terms(1, 7, 1)
    to_twin(1)

    def to_side(h):
        got(f"T{h}p", trecv.at[h, oxl], twin)
        xsend[h] = (total[h, oxl, core] * scale + trecv[h, oxl].astype(F32)).astype(BF16)
        put(f"X{h}", xsend.at[h], xrecv.at[h], side)

    to_side(1)
    add_terms(0, 7, 1)
    to_twin(0)
    to_side(0)
    for h in (1, 0):
        got(f"T{h}s", trecv.at[h, xl], twin)
        total[h, xl, core] = total[h, xl, core] * scale + trecv[h, xl].astype(F32)
    for h in (1, 0):
        got(f"X{h}", xrecv.at[h], side)
        final[:, pl.ds(h * R, R)] = total[h, xl, core] + xrecv[h].astype(F32)
    store = pltpu.make_async_copy(final, ag_h.at[0], lsem.at[6])
    store.start()

    for step in range(1, NZ):
        spread_norm(step).wait_send()
    for copy in pending:
        copy.wait_send()

    @pl.when(sec <= 1)
    def _():
        tour_sent("Ha", hidden, gather_h, 0, ROWS)

    @pl.when(sec > 1)
    def _():
        tour_sent("Ad", acts, gather_a, 0, ROWS)
        tour_sent("Hb", hidden, gather_h, 0, ROWS)

    def settle(i, carry):
        @pl.when(sec > 0)
        def _():
            for n in range(NZ):
                hop(i, n, res).wait_send()

        for n in range(NZ - 1):
            spread_grad(i, n, z).wait_send()

        @pl.when(sec <= 1)
        def _():
            for n in range(NZ - 1):
                spread_act(i, n, z).wait_send()

        keep(i).wait()
        return carry

    lax.fori_loop(0, NBLK, settle, 0)
    store.wait()
    assert len(names) <= NSEM


def per_device(*arrays):
    vmem = pl.BlockSpec(memory_space=pltpu.VMEM)
    smem = pl.BlockSpec(memory_space=pltpu.SMEM)
    hbm = pl.BlockSpec(memory_space=pl.ANY)
    return pl.pallas_call(
        kernel,
        out_shape=(
            jax.ShapeDtypeStruct((1, 2, TOK, D), BF16),
            jax.ShapeDtypeStruct((1, SHARD, 2 * R), F32),
        ),
        in_specs=[hbm, hbm, vmem, smem, hbm, vmem, vmem, hbm, hbm],
        out_specs=(hbm, hbm),
        scratch_shapes=[
            pltpu.VMEM((2, TOK, D), BF16),
            pltpu.VMEM((2, TOK, D), jnp.int32),
            pltpu.VMEM((ROWS, D), BF16),
            pltpu.VMEM((ROWS + BLK, D), BF16),
            pltpu.VMEM((NZ, 2, 2, SHARD, R), BF16),
            pltpu.VMEM((NZ, 2, 2, SHARD, R), BF16),
            pltpu.VMEM((ROWS, D), BF16),
            pltpu.VMEM((ROWS, D), BF16),
            pltpu.VMEM((ROWS + BLK, R), F32),
            pltpu.VMEM((ROWS, R), F32),
            pltpu.VMEM((ROWS, R), F32),
            pltpu.VMEM((1, R), F32),
            pltpu.VMEM((ROWS, R), BF16),
            pltpu.VMEM((ROWS, R), BF16),
            pltpu.VMEM((ROWS, 1), F32),
            pltpu.VMEM((ROWS, 1), F32),
            pltpu.VMEM((ROWS, 1), F32),
            pltpu.VMEM((NZ, ROWS, QUAD), BF16),
            pltpu.VMEM((NZ, ROWS, QUAD), BF16),
            pltpu.VMEM((NZ, ROWS, R), BF16),
            pltpu.VMEM((NZ, ROWS, R), BF16),
            pltpu.VMEM((2, 2, 2, SHARD, R), F32),
            pltpu.VMEM((2, 2, SHARD, R), BF16),
            pltpu.VMEM((2, 2, SHARD, R), BF16),
            pltpu.VMEM((2, SHARD, R), BF16),
            pltpu.VMEM((2, SHARD, R), BF16),
            pltpu.VMEM((SHARD, 2 * R), F32),
            pltpu.SemaphoreType.DMA((NSEM,)),
            pltpu.SemaphoreType.DMA((NSEM,)),
            pltpu.SemaphoreType.DMA((NBLK * NZ,)),
            pltpu.SemaphoreType.DMA((NBLK * NZ,)),
            pltpu.SemaphoreType.DMA((NBLK * NZ,)),
            pltpu.SemaphoreType.DMA((NBLK * NZ,)),
            pltpu.SemaphoreType.DMA((NBLK * NZ,)),
            pltpu.SemaphoreType.DMA((NBLK * NZ,)),
            pltpu.SemaphoreType.DMA((NBLK,)),
            pltpu.SemaphoreType.DMA((8,)),
        ],
        compiler_params=pltpu.CompilerParams(
            collective_id=0, has_side_effects=True, vmem_limit_bytes=60 << 20
        ),
        cost_estimate=pl.CostEstimate(
            flops=10 * ROWS * D * R, bytes_accessed=24 << 20, transcendentals=2 * ROWS * R
        ),
    )(*arrays)


def solution(mesh):
    return jax.shard_map(
        per_device,
        mesh=mesh,
        in_specs=(
            P("section", "rep", None, None),
            P("section", "rep", None, None),
            P("section", "rep", None),
            P("rep", None),
            P("rep", None, None),
            P("section", None),
            P("section", None),
            P("section", "rep", None),
            P("section", "rep", None),
        ),
        out_specs=(P("section", "rep", None, None), P("section", "rep", None)),
        check_vma=False,
    )
```
